128 devices in a mesh: dp: 4 (over x), ctx: 32 (over z, y, core).
Axes of the slice: x: 4, y: 4, z: 4, core: 2. Of those that a mesh axis runs over, the one named last changes fastest.
Arguments:
- queries: bfloat16 [4, 4096, 4096], P('dp', 'ctx'), may hold values from -9.5 to 9.5
- keys: bfloat16 [4, 4096, 512], P('dp', 'ctx'), may hold values from -6 to 6
- values: bfloat16 [4, 4096, 512], P('dp', 'ctx'), may hold values from -6 to 6
- out_grad: bfloat16 [4, 4096, 4096], P('dp', 'ctx'), may hold values from -6 to 6
- segment_ids: int32 [4, 4096], P('dp', 'ctx'), may hold values from 0 to 3, never falling along the last dimension, each value on 1 to 2048 neighbouring positions
- loss_mask: int32 [4, 4096], P('dp', 'ctx'), may hold values from 0 to 1, as said below
Outputs:
- attn_out: bfloat16 [4, 4096, 4096], P('dp', 'ctx')
- q_grad: bfloat16 [4, 4096, 4096], P('dp', 'ctx')
- k_grad: bfloat16 [4, 4096, 512], P('dp', 'ctx')
- v_grad: bfloat16 [4, 4096, 512], P('dp', 'ctx')
The draws below stay inside these ranges and needn't reach their ends.
Inputs may be any that keep to these rules, and one draw needn't show every extreme that they name: `segment_ids`: document numbers never fall along a sequence; each document holds 1 to 2048 tokens and one holds exactly 2048. `loss_mask`: the last token of every sequence counts.
All inputs are finite; a program needn't handle non-finite values.
Results may differ from the reference program's by a relative error of at most 0.024.
Values may be sent and summed in bfloat16 or wider, within the bound.
No kernel may reach another device: no remote copies, remote signals or barrier semaphores. Data moves between devices by JAX's collectives and lax.ppermute only.
A program may use at most 128 MiB of HBM per device.

```python
import math
from functools import partial
import jax
import jax.numpy as jnp
import numpy as np
from jax import lax

QUERY_HEADS = 32
KEY_VALUE_HEADS = 4
HEAD_SIZE = 128
PACKED_LENGTH = 4096
PACKED_SEQUENCES = 4
DOCS = 4
DOC_MOST = 2048


def draw_queries(key, part):
    key = jax.random.fold_in(key, 7)
    sampled_values = jax.random.truncated_normal(key, -6.0, 6.0, (PACKED_SEQUENCES, PACKED_LENGTH, QUERY_HEADS, HEAD_SIZE), jnp.float32)
    return sampled_values.reshape(PACKED_SEQUENCES, PACKED_LENGTH, QUERY_HEADS * HEAD_SIZE).astype(jnp.bfloat16)


def draw_keys(key, part):
    key = jax.random.fold_in(key, 11)
    sampled_values = jax.random.truncated_normal(key, -6.0, 6.0, (PACKED_SEQUENCES, PACKED_LENGTH, KEY_VALUE_HEADS, HEAD_SIZE), jnp.float32)
    return sampled_values.reshape(PACKED_SEQUENCES, PACKED_LENGTH, KEY_VALUE_HEADS * HEAD_SIZE).astype(jnp.bfloat16)


def draw_loss_mask(key, part):
    key = jax.random.fold_in(key, 23)
    order = jnp.arange(PACKED_SEQUENCES, dtype=jnp.int32)[:, None] * PACKED_LENGTH + jnp.arange(PACKED_LENGTH, dtype=jnp.int32)[None, :]
    limit = 150 + 800 * order // (PACKED_SEQUENCES * PACKED_LENGTH)
    rolled = jax.random.randint(key, (PACKED_SEQUENCES, PACKED_LENGTH), 0, 1000)
    marked = (rolled < limit) | (jnp.arange(PACKED_LENGTH)[None, :] == PACKED_LENGTH - 1)
    return marked.astype(jnp.int32)


def block_scale(key, shape, shards, smallest, largest):
    def one(axis_at, parts):
        steps = jax.random.uniform(jax.random.fold_in(jax.random.fold_in(key, 6), axis_at), (parts,), jnp.float32, smallest / len(shards), largest / len(shards))
        return jnp.repeat(jnp.exp(steps), shape[axis_at] // parts).reshape((-1,) + (1,) * (len(shape) - axis_at - 1))

    level = one(*shards[0])
    for cut in shards[1:]:
        level = level * one(*cut)
    return level


def split_up(amount, total, bound, slope):
    weights = [(1 << 20) // math.isqrt(standing ** slope) + 1 for standing in range(2, amount + 1)]
    spare, counts = total - bound - (amount - 1), [1] * (amount - 1)
    while spare > 0:
        movable = [i for i in range(amount - 1) if counts[i] < bound]
        pool, remaining = sum([weights[i] for i in movable]), spare
        for i in movable:
            addition = min(bound - counts[i], max(1, remaining * weights[i] // pool), spare)
            counts[i] = counts[i] + addition
            spare = spare - addition
    return np.array([bound] + counts)


def uneven_parts(own_key, amount, total, reach, slope):
    if amount == 2:
        one = jax.random.randint(own_key, (), max(1, total - reach), min(reach, total - 1) + 1)
        return jnp.stack([one, total - one])
    lengths = jnp.asarray(split_up(amount, total, reach, slope), jnp.int32)
    pairs = (amount - 1) // 2
    donor, receiver = lengths[1:1 + 2 * pairs:2], lengths[2:2 + 2 * pairs:2]
    slack = jnp.minimum(donor - 1, reach - receiver)
    passed = jax.random.randint(jax.random.fold_in(own_key, 1), (pairs,), 0, 1 << 20) % (slack + 1)
    lengths = lengths.at[1:1 + 2 * pairs:2].set(donor - passed).at[2:2 + 2 * pairs:2].set(receiver + passed)
    return lengths[jax.random.permutation(jax.random.fold_in(own_key, 2), amount)]


def bell_draw(stream_key, shape, deviation, bound, shards=(), kind=jnp.bfloat16):
    result = deviation * jax.random.normal(stream_key, shape, jnp.float32)
    if shards:
        result = result * block_scale(stream_key, shape, shards, -0.22, 0.18)
    return jnp.clip(result, -bound, bound).astype(kind)


def setup_inputs(seed: int = 0) -> dict:
    seeds = jax.random.split(jax.random.key(seed), 7)
    return {
        "queries": draw_queries(jax.random.fold_in(seeds[6], 71), 0),
        "keys": draw_keys(jax.random.fold_in(seeds[6], 71), 0),
        "values": bell_draw(seeds[2], (PACKED_SEQUENCES, PACKED_LENGTH, KEY_VALUE_HEADS * HEAD_SIZE), 1.0, 6.0, ((0, 4), (1, 32))),
        "out_grad": bell_draw(seeds[3], (PACKED_SEQUENCES, PACKED_LENGTH, QUERY_HEADS * HEAD_SIZE), 1.0, 6.0, ((0, 4), (1, 32))),
        "segment_ids": jax.vmap(lambda own: jnp.searchsorted(jnp.cumsum(uneven_parts(own, DOCS, PACKED_LENGTH, DOC_MOST, 2)), jnp.arange(PACKED_LENGTH), side="right"))(jax.random.split(seeds[4], PACKED_SEQUENCES)).reshape((PACKED_SEQUENCES, PACKED_LENGTH)).astype(jnp.int32),
        "loss_mask": draw_loss_mask(jax.random.fold_in(seeds[6], 71), 0),
    }


NEG = -1e+30

def head_terms(allowed, scale_for_scores, operands):
    q_head, k_head, v_head, g_head = operands
    scores = jnp.dot(q_head, k_head.T, preferred_element_type=jnp.float32) * scale_for_scores
    scores = jnp.where(allowed, scores, NEG)
    row_top = lax.optimization_barrier(jnp.max(scores, axis=1, keepdims=True))
    log_total = row_top + jnp.log(lax.optimization_barrier(jnp.sum(jnp.exp(scores - row_top), axis=1, keepdims=True)))
    probs = jnp.exp(scores - log_total)
    weights = probs.astype(jnp.bfloat16)
    attn = jnp.dot(weights, v_head, preferred_element_type=jnp.float32).astype(jnp.bfloat16)
    row_delta = lax.optimization_barrier(jnp.sum(attn.astype(jnp.float32) * g_head.astype(jnp.float32), axis=1, keepdims=True))
    dweights = jnp.dot(g_head, v_head.T, preferred_element_type=jnp.float32)
    dscores = (probs * (dweights - row_delta)).astype(jnp.bfloat16)
    dquery = jnp.dot(dscores, k_head, preferred_element_type=jnp.float32) * scale_for_scores
    key_gradient = jnp.dot(dscores.T, q_head, preferred_element_type=jnp.float32)
    value_gradient = jnp.dot(weights.T, g_head, preferred_element_type=jnp.float32)
    return (attn, dquery, key_gradient, value_gradient)

def sequence_pass(query_rows, key_row_block, value_row_block, grad_rows, doc_ids):
    sequence_rows = query_rows.shape[0]
    grouped_heads = QUERY_HEADS // KEY_VALUE_HEADS
    scale_for_scores = 1.0 / math.sqrt(HEAD_SIZE)
    positions = jnp.arange(sequence_rows, dtype=jnp.int32)
    allowed = (positions[None, :] <= positions[:, None]) & (doc_ids[None, :] == doc_ids[:, None])
    query_heads = query_rows.reshape(sequence_rows, QUERY_HEADS, HEAD_SIZE).transpose(1, 0, 2)
    gradient_heads = grad_rows.reshape(sequence_rows, QUERY_HEADS, HEAD_SIZE).transpose(1, 0, 2)
    key_heads = jnp.repeat(key_row_block.reshape(sequence_rows, KEY_VALUE_HEADS, HEAD_SIZE).transpose(1, 0, 2), grouped_heads, axis=0)
    value_heads = jnp.repeat(value_row_block.reshape(sequence_rows, KEY_VALUE_HEADS, HEAD_SIZE).transpose(1, 0, 2), grouped_heads, axis=0)
    attn, dquery, key_gradient, value_gradient = lax.map(partial(head_terms, allowed, scale_for_scores), (query_heads, key_heads, value_heads, gradient_heads))
    attn = attn.transpose(1, 0, 2).reshape(sequence_rows, QUERY_HEADS * HEAD_SIZE)
    dquery = dquery.astype(jnp.bfloat16).transpose(1, 0, 2).reshape(sequence_rows, QUERY_HEADS * HEAD_SIZE)
    key_gradient = (lax.optimization_barrier(jnp.sum(key_gradient.reshape(KEY_VALUE_HEADS, grouped_heads, sequence_rows, HEAD_SIZE), axis=1)) * scale_for_scores).astype(jnp.bfloat16)
    value_gradient = lax.optimization_barrier(jnp.sum(value_gradient.reshape(KEY_VALUE_HEADS, grouped_heads, sequence_rows, HEAD_SIZE), axis=1)).astype(jnp.bfloat16)
    key_gradient = key_gradient.transpose(1, 0, 2).reshape(sequence_rows, KEY_VALUE_HEADS * HEAD_SIZE)
    value_gradient = value_gradient.transpose(1, 0, 2).reshape(sequence_rows, KEY_VALUE_HEADS * HEAD_SIZE)
    return (attn, dquery, key_gradient, value_gradient)

def reference(queries, keys, values, out_grad, segment_ids, loss_mask):
    weight = loss_mask.astype(jnp.float32)
    counted = jnp.sum(weight)
    scaled = (out_grad.astype(jnp.float32) * weight[:, :, None] * float(PACKED_SEQUENCES * PACKED_LENGTH) / counted).astype(jnp.bfloat16)
    results = [sequence_pass(queries[b], keys[b], values[b], scaled[b], segment_ids[b]) for b in range(PACKED_SEQUENCES)]
    attn_out = jnp.stack([r[0] for r in results])
    q_grad = jnp.stack([r[1] for r in results])
    k_grad = jnp.stack([r[2] for r in results])
    v_grad = jnp.stack([r[3] for r in results])
    return (attn_out, q_grad, k_grad, v_grad)
```

```python
import math, functools
import jax, jax.numpy as jnp
from jax import lax
from jax.sharding import PartitionSpec as P
from jax.experimental import pallas as pl
from jax.experimental.pallas import tpu as pltpu

NEG = -1e30
CH = math.log2(math.e) / math.sqrt(128)
BF, F32 = jnp.bfloat16, jnp.float32
NB = 9
NT = (((1,), (1,)), ((), ()))


def mm(a, b):
    return jnp.dot(a, b, preferred_element_type=F32)


def mmt(a, b):
    return lax.dot_general(a, b, NT, preferred_element_type=F32)


def attend_kernel(s_ref, qo_ref, qs_ref, go_ref, gs_ref, own_ref, za_ref, zc_ref, y1_ref, y2_ref, y3_ref,
                  oo_ref, os_ref, dqo_ref, dqs_ref, p1_ref, p2_ref, p3_ref, loc_ref,
                  kk, vv, kt, vt, bias, sc, pp, ds, dka, dva):
    core, z, y = s_ref[0], s_ref[1], s_ref[2]
    chip = 4 * z + y
    blocks = [(own_ref, (), None), (za_ref, (), chip - 4), (zc_ref, (), chip - 8)]
    for s, r in ((1, y1_ref), (2, y2_ref), (3, y3_ref)):
        turned = lax.rem(y - s + 4, 4)
        blocks.append((r, (0,), 4 * z - 4 + turned))
        blocks.append((r, (1,), chip - s - jnp.where(y >= s, 0, 4)))
    lane = lax.broadcasted_iota(jnp.int32, (1, 128), 1)
    t_seg = jnp.concatenate([own_ref[0, 256:257], own_ref[1, 256:257]], axis=1).astype(F32)
    t_mask = jnp.concatenate([own_ref[0, 257:258], own_ref[1, 257:258]], axis=1).astype(F32)
    t_pos = jnp.concatenate([core * 128 + lane, (1 - core) * 128 + lane], axis=1)
    key = lax.broadcasted_iota(jnp.int32, (128, 256), 0)
    for b, (ref, pre, idx) in enumerate(blocks):
        for o in range(2):
            r0 = b * 256 + o * 128
            k = ref[pre + (o, slice(0, 128))]
            v = ref[pre + (o, slice(128, 256))]
            kk[r0:r0 + 128] = k
            vv[r0:r0 + 128] = v
            kt[:, r0:r0 + 128] = k.T
            vt[:, r0:r0 + 128] = v.T
            k_seg = ref[pre + (o, slice(256, 257))].astype(F32)
            n = [jnp.sum((k_seg < s).astype(F32), axis=1, keepdims=True) for s in (1, 2, 3)]
            first = jnp.where(t_seg == 3, n[2], jnp.where(t_seg == 2, n[1], jnp.where(t_seg == 1, n[0], 0.0)))
            first = first.astype(jnp.int32)
            if idx is None:
                at = core * 128 if o == 0 else (1 - core) * 128
                ok = (key >= first) & (key + at <= t_pos)
            else:
                first = jnp.where(idx >= 0, first, 128)
                ok = key >= first
            bias[r0:r0 + 128] = jnp.where(ok, 0.0, NEG)
    dka[...] = jnp.zeros_like(dka)
    dva[...] = jnp.zeros_like(dva)

    def head(h, _):
        cols = pl.ds(pl.multiple_of(h * 128, 128), 128)
        q = jnp.concatenate([qo_ref[:, cols], qs_ref[:, cols]], axis=0)
        g = jnp.concatenate([go_ref[:, cols], gs_ref[:, cols]], axis=0)
        top = jnp.full((8, 256), NEG, F32)
        for b in range(NB):
            rows = slice(b * 256, b * 256 + 256)
            s = mmt(kk[rows], q) + bias[rows]
            sc[rows] = s
            top = jnp.maximum(top, jnp.max(s.reshape(32, 8, 256), axis=0))
        top = jnp.max(top, axis=0, keepdims=True) * CH
        mass = jnp.zeros((8, 256), F32)
        for b in range(NB):
            rows = slice(b * 256, b * 256 + 256)
            p = jnp.exp2(sc[rows] * CH - top)
            mass = mass + jnp.sum(p.reshape(32, 8, 256), axis=0)
            pp[rows] = p.astype(BF)
        inv = 1.0 / jnp.sum(mass, axis=0, keepdims=True)
        ot = (mm(vt[...], pp[...]) * inv).astype(BF)
        out = ot.T
        oo_ref[:, cols] = out[:128]
        os_ref[:, cols] = out[128:]
        delta = jnp.sum(ot.astype(F32) * g.T.astype(F32), axis=0, keepdims=True)
        inv = inv * t_mask
        col = jnp.broadcast_to(inv, (128, 256)).T
        qn = (q.astype(F32) * col).astype(BF)
        gn = (g.astype(F32) * col).astype(BF)
        for b in range(NB):
            rows = slice(b * 256, b * 256 + 256)
            p = pp[rows]
            d = (p.astype(F32) * (mmt(vv[rows], g) - delta)).astype(BF)
            ds[rows] = d
            dva[rows] += mm(p, gn)
            dka[rows] += mm(d, qn)
        dq = (mm(kt[...], ds[...]) * (inv * (1.0 / math.sqrt(128)))).astype(BF).T
        dqo_ref[:, cols] = dq[:128]
        dqs_ref[:, cols] = dq[128:]
        return 0

    lax.fori_loop(0, 8, head, 0)
    for b in range(NB):
        for o in range(2):
            rows = slice(b * 256 + o * 128, b * 256 + o * 128 + 128)
            if b < 3:
                loc_ref[b, o, 0] = dka[rows]
                loc_ref[b, o, 1] = dva[rows]
            else:
                ref = (p1_ref, p2_ref, p3_ref)[(b - 3) // 2]
                ref[(b - 3) % 2, o, 0] = dka[rows].astype(BF)
                ref[(b - 3) % 2, o, 1] = dva[rows].astype(BF)


def attend(scal, j, q, qs, g, gs, own, za, zc, y1, y2, y3):
    wide = lambda f: pl.BlockSpec((128, 1024), f)
    whole = lambda a: pl.BlockSpec(a.shape, lambda i, s, n=a.ndim: (0,) * n)
    mine = wide(lambda i, s: (0, s[0] * 2 + j))
    other = wide(lambda i, s: (0, j))
    rows = jax.ShapeDtypeStruct((128, 1024), BF)
    part = jax.ShapeDtypeStruct((2, 2, 2, 128, 128), BF)
    loc = jax.ShapeDtypeStruct((3, 2, 2, 128, 128), F32)
    outs = [rows] * 4 + [part] * 3 + [loc]
    n = NB * 256
    return pl.pallas_call(
        attend_kernel,
        out_shape=outs,
        grid_spec=pltpu.PrefetchScalarGridSpec(
            num_scalar_prefetch=1,
            grid=(1,),
            in_specs=[mine, other, mine, other] + [whole(a) for a in (own, za, zc, y1, y2, y3)],
            out_specs=[whole(o) for o in outs],
            scratch_shapes=[
                pltpu.VMEM((n, 128), BF), pltpu.VMEM((n, 128), BF), pltpu.VMEM((128, n), BF), pltpu.VMEM((128, n), BF),
                pltpu.VMEM((n, 256), F32), pltpu.VMEM((n, 256), F32), pltpu.VMEM((n, 256), BF), pltpu.VMEM((n, 256), BF),
                pltpu.VMEM((n, 128), F32), pltpu.VMEM((n, 128), F32),
            ],
        ),
        compiler_params=pltpu.CompilerParams(vmem_limit_bytes=48 * 2**20),
        name="attend",
    )(scal, q, qs, g, gs, own, za, zc, y1, y2, y3)


def shard(queries, keys, values, out_grad, segment_ids, loss_mask):
    me = lax.axis_index("ctx")
    core, y, z = me % 2, me // 2 % 4, me // 8
    q, k, v, g = queries[0], keys[0], values[0], out_grad[0]

    def send(x, target):
        pairs = []
        for i in range(32):
            zz, yy, cc = target(i // 8, i // 2 % 4, i % 2)
            if 0 <= zz < 4:
                pairs.append((i, (zz * 4 + yy % 4) * 2 + cc % 2))
        return lax.ppermute(x, "ctx", pairs)

    swap = lambda x: send(x, lambda z, y, c: (z, y, c + 1))
    along_z = lambda x, a: send(x, lambda z, y, c: (z + a, y, c))
    along_y = lambda x, s: send(x, lambda z, y, c: (z, y + s, c))

    counted = jnp.sum(loss_mask.astype(F32), axis=1, keepdims=True)
    counted = counted + swap(counted)
    for step in (1, 2):
        counted = counted + lax.ppermute(counted, "dp", [(i, i ^ step) for i in range(4)])
        counted = counted + send(counted, lambda z, y, c: (z, y ^ step, c))
        counted = counted + send(counted, lambda z, y, c: (z ^ step, y, c))

    info = jnp.concatenate([segment_ids.astype(BF), loss_mask.astype(BF), jnp.zeros((14, 128), BF)], axis=0)

    def payload(c):
        heads = lambda a: lax.dynamic_slice(a, (0, c * 256), (128, 256)).reshape(128, 2, 128).transpose(1, 0, 2)
        return jnp.concatenate([heads(k), heads(v), jnp.broadcast_to(info, (2, 16, 128))], axis=1)

    own = jnp.stack([payload(core), swap(payload(1 - core))], axis=1)
    half = lambda a, c: lax.dynamic_slice(a, (0, c * 2048), (128, 2048))
    za, zc = along_z(own, 1), along_z(own, 2)
    qs, gs = swap(half(q, 1 - core)), swap(half(g, 1 - core))
    scal = jnp.stack([core, z, y]).astype(jnp.int32)

    ys = []
    for j in range(2):
        ys.append([
            along_y(jnp.stack([za[j], jnp.where(y + s < 4, own[j], zc[j])]), s) for s in (1, 2, 3)
        ])
    rows_out, grads = [], []
    for j in range(2):
        oo, os, dqo, dqs, p1, p2, p3, loc = attend(scal, j, q, qs, g, gs, own[j], za[j], zc[j], *ys[j])
        rows_out.append((oo, dqo, swap(jnp.stack([os, dqs]))))
        got = [along_y(p, -s) for s, p in ((1, p1), (2, p2), (3, p3))]
        got = [a.astype(F32) for a in got]
        back_a, back_c, here = loc[1], loc[2], loc[0]
        for s in (1, 2, 3):
            a = got[s - 1]
            back_a = back_a + a[0]
            here = here + jnp.where(y + s < 4, a[1], 0.0)
            back_c = back_c + jnp.where(y + s < 4, 0.0, a[1])
        grads.append(here + along_z(back_a.astype(BF), -1).astype(F32) + along_z(back_c.astype(BF), -2).astype(F32))
    scale = float(lax.axis_size("dp") * 4096) / counted[0, 0]
    total = jnp.stack(grads) * (jnp.array([1.0 / math.sqrt(128), 1.0], F32)[None, None, :, None, None] * scale)
    total = total.astype(BF)
    mine, theirs = total[:, 0], swap(total[:, 1])

    def join(a, b, axis):
        return jnp.concatenate([jnp.where(core == 0, a, b), jnp.where(core == 0, b, a)], axis=axis)

    both = join(mine, theirs, 0).transpose(1, 2, 0, 3).reshape(2, 128, 512)
    attn = join(jnp.concatenate([r[0] for r in rows_out], 1), jnp.concatenate([r[2][0] for r in rows_out], 1), 1)
    dq = join(jnp.concatenate([r[1] for r in rows_out], 1), jnp.concatenate([r[2][1] for r in rows_out], 1), 1)
    dq = (dq.astype(F32) * scale).astype(BF)
    return attn[None], dq[None], both[0][None], both[1][None]


def solution(mesh):
    rows, ids = P("dp", "ctx", None), P("dp", "ctx")
    return jax.shard_map(
        shard, mesh=mesh, in_specs=(rows,) * 4 + (ids,) * 2, out_specs=(rows,) * 4, check_vma=False
    )
```

```python
import math, functools
import jax, jax.numpy as jnp
from jax import lax
from jax.sharding import PartitionSpec as P
from jax.experimental import pallas as pl
from jax.experimental.pallas import tpu as pltpu

NEG = -1e30
CH = math.log2(math.e) / math.sqrt(128)
BF, F32 = jnp.bfloat16, jnp.float32
NB = 9
NT = (((1,), (1,)), ((), ()))


def mm(a, b):
    return jnp.dot(a, b, preferred_element_type=F32)


def mmt(a, b):
    return lax.dot_general(a, b, NT, preferred_element_type=F32)


def attend_kernel(s_ref, qo_ref, qs_ref, go_ref, gs_ref, own_ref, za_ref, zc_ref, y1_ref, y2_ref, y3_ref, tally_ref,
                  oo_ref, os_ref, dqo_ref, dqs_ref, p1_ref, p2_ref, p3_ref, loc_ref, cnt_ref,
                  kk, vv, kt, vt, bias, sc, pp, ds, dka, dva):
    core, z, y = s_ref[0], s_ref[1], s_ref[2]
    chip = 4 * z + y
    blocks = [(own_ref, (), None), (za_ref, (), chip - 4), (zc_ref, (), chip - 8)]
    for s, r in ((1, y1_ref), (2, y2_ref), (3, y3_ref)):
        turned = lax.rem(y - s + 4, 4)
        blocks.append((r, (0,), 4 * z - 4 + turned))
        blocks.append((r, (1,), chip - s - jnp.where(y >= s, 0, 4)))
    lane = lax.broadcasted_iota(jnp.int32, (1, 128), 1)
    t_seg = jnp.concatenate([own_ref[0, 256:257], own_ref[1, 256:257]], axis=1).astype(F32)
    t_mask = jnp.concatenate([own_ref[0, 257:258], own_ref[1, 257:258]], axis=1).astype(F32)
    t_pos = jnp.concatenate([core * 128 + lane, (1 - core) * 128 + lane], axis=1)
    key = lax.broadcasted_iota(jnp.int32, (128, 256), 0)
    for b, (ref, pre, idx) in enumerate(blocks):
        for o in range(2):
            r0 = b * 256 + o * 128
            k = ref[pre + (o, slice(0, 128))]
            v = ref[pre + (o, slice(128, 256))]
            kk[r0:r0 + 128] = k
            vv[r0:r0 + 128] = v
            kt[:, r0:r0 + 128] = k.T
            vt[:, r0:r0 + 128] = v.T
            k_seg = ref[pre + (o, slice(256, 257))].astype(F32)
            n = [jnp.sum((k_seg < s).astype(F32), axis=1, keepdims=True) for s in (1, 2, 3)]
            first = jnp.where(t_seg == 3, n[2], jnp.where(t_seg == 2, n[1], jnp.where(t_seg == 1, n[0], 0.0)))
            first = first.astype(jnp.int32)
            if idx is None:
                at = core * 128 if o == 0 else (1 - core) * 128
                ok = (key >= first) & (key + at <= t_pos)
            else:
                first = jnp.where(idx >= 0, first, 128)
                ok = key >= first
            bias[r0:r0 + 128] = jnp.where(ok, 0.0, NEG)
    tally = tally_ref[...]
    for ref in (y1_ref, y2_ref, y3_ref):
        tally = tally + 32.0 * ref[0, 0, 258:259].astype(F32) + ref[0, 0, 259:260].astype(F32)
    cnt_ref[...] = tally
    dka[...] = jnp.zeros_like(dka)
    dva[...] = jnp.zeros_like(dva)

    def head(h, _):
        cols = pl.ds(pl.multiple_of(h * 128, 128), 128)
        q = jnp.concatenate([qo_ref[:, cols], qs_ref[:, cols]], axis=0)
        g = jnp.concatenate([go_ref[:, cols], gs_ref[:, cols]], axis=0)
        top = jnp.full((8, 256), NEG, F32)
        for b in range(NB):
            rows = slice(b * 256, b * 256 + 256)
            s = mmt(kk[rows], q) + bias[rows]
            sc[rows] = s
            top = jnp.maximum(top, jnp.max(s.reshape(32, 8, 256), axis=0))
        top = jnp.max(top, axis=0, keepdims=True) * CH
        mass = jnp.zeros((8, 256), F32)
        for b in range(NB):
            rows = slice(b * 256, b * 256 + 256)
            p = jnp.exp2(sc[rows] * CH - top)
            mass = mass + jnp.sum(p.reshape(32, 8, 256), axis=0)
            pp[rows] = p.astype(BF)
        inv = 1.0 / jnp.sum(mass, axis=0, keepdims=True)
        ot = (mm(vt[...], pp[...]) * inv).astype(BF)
        out = ot.T
        oo_ref[:, cols] = out[:128]
        os_ref[:, cols] = out[128:]
        delta = jnp.sum(ot.astype(F32) * g.T.astype(F32), axis=0, keepdims=True)
        inv = inv * t_mask
        col = jnp.broadcast_to(inv, (128, 256)).T
        qn = (q.astype(F32) * col).astype(BF)
        gn = (g.astype(F32) * col).astype(BF)
        for b in range(NB):
            rows = slice(b * 256, b * 256 + 256)
            p = pp[rows]
            d = (p.astype(F32) * (mmt(vv[rows], g) - delta)).astype(BF)
            ds[rows] = d
            dva[rows] += mm(p, gn)
            dka[rows] += mm(d, qn)
        dq = (mm(kt[...], ds[...]) * (inv * (1.0 / math.sqrt(128)))).astype(BF).T
        dqo_ref[:, cols] = dq[:128]
        dqs_ref[:, cols] = dq[128:]
        return 0

    lax.fori_loop(0, 8, head, 0)
    for b in range(NB):
        for o in range(2):
            rows = slice(b * 256 + o * 128, b * 256 + o * 128 + 128)
            if b < 3:
                loc_ref[b, o, 0] = dka[rows]
                loc_ref[b, o, 1] = dva[rows]
            else:
                ref = (p1_ref, p2_ref, p3_ref)[(b - 3) // 2]
                ref[(b - 3) % 2, o, 0] = dka[rows].astype(BF)
                ref[(b - 3) % 2, o, 1] = dva[rows].astype(BF)


def attend(scal, j, q, qs, g, gs, own, za, zc, y1, y2, y3, tally):
    wide = lambda f: pl.BlockSpec((128, 1024), f)
    whole = lambda a: pl.BlockSpec(a.shape, lambda i, s, n=a.ndim: (0,) * n)
    mine = wide(lambda i, s: (0, s[0] * 2 + j))
    other = wide(lambda i, s: (0, j))
    rows = jax.ShapeDtypeStruct((128, 1024), BF)
    part = jax.ShapeDtypeStruct((2, 2, 2, 128, 128), BF)
    loc = jax.ShapeDtypeStruct((3, 2, 2, 128, 128), F32)
    outs = [rows] * 4 + [part] * 3 + [loc, jax.ShapeDtypeStruct((8, 128), F32)]
    n = NB * 256
    return pl.pallas_call(
        attend_kernel,
        out_shape=outs,
        grid_spec=pltpu.PrefetchScalarGridSpec(
            num_scalar_prefetch=1,
            grid=(1,),
            in_specs=[mine, other, mine, other] + [whole(a) for a in (own, za, zc, y1, y2, y3, tally)],
            out_specs=[whole(o) for o in outs],
            scratch_shapes=[
                pltpu.VMEM((n, 128), BF), pltpu.VMEM((n, 128), BF), pltpu.VMEM((128, n), BF), pltpu.VMEM((128, n), BF),
                pltpu.VMEM((n, 256), F32), pltpu.VMEM((n, 256), F32), pltpu.VMEM((n, 256), BF), pltpu.VMEM((n, 256), BF),
                pltpu.VMEM((n, 128), F32), pltpu.VMEM((n, 128), F32),
            ],
        ),
        compiler_params=pltpu.CompilerParams(vmem_limit_bytes=48 * 2**20),
        cost_estimate=pl.CostEstimate(flops=15 * 2**30, bytes_accessed=4 * 2**20, transcendentals=5 * 2**20),
        name="attend",
    )(scal, q, qs, g, gs, own, za, zc, y1, y2, y3, tally)


def shard(queries, keys, values, out_grad, segment_ids, loss_mask):
    me = lax.axis_index("ctx")
    core, y, z = me % 2, me // 2 % 4, me // 8
    q, k, v, g = queries[0], keys[0], values[0], out_grad[0]

    def send(x, target, turn=False):
        pairs = []
        for i in range(32):
            zz, yy, cc = target(i // 8, i // 2 % 4, i % 2)
            if turn or 0 <= zz < 4:
                pairs.append((i, (zz % 4 * 4 + yy % 4) * 2 + cc % 2))
        return lax.ppermute(x, "ctx", pairs)

    swap = lambda x: send(x, lambda z, y, c: (z, y, c + 1))
    along_z = lambda x, a, turn=False: send(x, lambda z, y, c: (z + a, y, c), turn)
    along_y = lambda x, s: send(x, lambda z, y, c: (z, y + s, c))

    info = jnp.concatenate([segment_ids.astype(BF), loss_mask.astype(BF), jnp.zeros((14, 128), BF)], axis=0)

    def payload(c):
        heads = lambda a: lax.dynamic_slice(a, (0, c * 256), (128, 256)).reshape(128, 2, 128).transpose(1, 0, 2)
        return jnp.concatenate([heads(k), heads(v), jnp.broadcast_to(info, (2, 16, 128))], axis=1)

    own = jnp.stack([payload(core), swap(payload(1 - core))], axis=1)
    half = lambda a, c: lax.dynamic_slice(a, (0, c * 2048), (128, 2048))
    za, zc = zip(*[(along_z(own[j], 1, True), along_z(own[j], 2)) for j in range(2)])
    qs, gs = swap(half(q, 1 - core)), swap(half(g, 1 - core))
    scal = jnp.stack([core, z, y]).astype(jnp.int32)

    counted = jnp.broadcast_to(jnp.sum(za[0][:, 257].astype(F32)), (8, 128))
    for step in (1, 2):
        counted = counted + lax.ppermute(counted, "dp", [(i, i ^ step) for i in range(4)])
    high = jnp.floor(counted[:1] / 32)
    digits = jnp.concatenate([high, counted[:1] - 32 * high]).astype(BF)

    ys = []
    for j in range(2):
        above = za[j] if j == 0 else za[j].at[0, 258:260].set(digits)
        ys.append([
            along_y(jnp.stack([above, jnp.where(y + s < 4, own[j], zc[j])]), s) for s in (1, 2, 3)
        ])
    rows_out, grads = [], []
    for j in range(2):
        oo, os, dqo, dqs, p1, p2, p3, loc, tally = attend(
            scal, j, q, qs, g, gs, own[j], za[j], zc[j], *ys[j], counted
        )
        rows_out.append((oo, dqo, swap(jnp.stack([os, dqs]))))
        got = [along_y(p, -s) for s, p in ((1, p1), (2, p2), (3, p3))]
        got = [a.astype(F32) for a in got]
        back_a, back_c, here = loc[1], loc[2], loc[0]
        for s in (1, 2, 3):
            a = got[s - 1]
            back_a = back_a + a[0]
            here = here + jnp.where(y + s < 4, a[1], 0.0)
            back_c = back_c + jnp.where(y + s < 4, 0.0, a[1])
        grads.append(here + along_z(back_a.astype(BF), -1).astype(F32) + along_z(back_c.astype(BF), -2).astype(F32))
    counted = tally
    for step in (1, 2):
        counted = counted + send(counted, lambda z, y, c: (z ^ step, y, c))
    scale = float(lax.axis_size("dp") * 4096) / counted[0, 0]
    total = jnp.stack(grads) * (jnp.array([1.0 / math.sqrt(128), 1.0], F32)[None, None, :, None, None] * scale)
    total = total.astype(BF)
    mine, theirs = total[:, 0], swap(total[:, 1])

    def join(a, b, axis):
        return jnp.concatenate([jnp.where(core == 0, a, b), jnp.where(core == 0, b, a)], axis=axis)

    both = join(mine, theirs, 0).transpose(1, 2, 0, 3).reshape(2, 128, 512)
    attn = join(jnp.concatenate([r[0] for r in rows_out], 1), jnp.concatenate([r[2][0] for r in rows_out], 1), 1)
    dq = join(jnp.concatenate([r[1] for r in rows_out], 1), jnp.concatenate([r[2][1] for r in rows_out], 1), 1)
    dq = (dq.astype(F32) * scale).astype(BF)
    return attn[None], dq[None], both[0][None], both[1][None]


def solution(mesh):
    rows, ids = P("dp", "ctx", None), P("dp", "ctx")
    return jax.shard_map(
        shard, mesh=mesh, in_specs=(rows,) * 4 + (ids,) * 2, out_specs=(rows,) * 4, check_vma=False
    )
```

```python
import math, functools
import jax, jax.numpy as jnp
from jax import lax
from jax.sharding import PartitionSpec as P
from jax.experimental import pallas as pl
from jax.experimental.pallas import tpu as pltpu

NEG = -1e30
CH = math.log2(math.e) / math.sqrt(128)
BF, F32 = jnp.bfloat16, jnp.float32
NB = 9
NT = (((1,), (1,)), ((), ()))


def mm(a, b):
    return jnp.dot(a, b, preferred_element_type=F32)


def mmt(a, b):
    return lax.dot_general(a, b, NT, preferred_element_type=F32)


def run_heads(score, weigh, output, dscore, dvalue, dkey, dquery, start):
    R = range(NB)
    S = [start(h) for h in range(8)]
    for b in R: score(0, S[0], b)
    for b in R: weigh(0, S[0], b)
    for b in R: score(1, S[1], b)
    for h in range(8):
        t, u = h % 2, (h + 1) % 2
        n = S[h + 1] if h < 7 else None
        n2 = S[h + 2] if h < 6 else None
        output(t, S[h])
        for b in R:
            dscore(t, S[h], b)
            if n: weigh(u, n, b)
        for b in R:
            dvalue(t, S[h], b); dkey(t, S[h], b)
            if n2: score(t, n2, b)
        dquery(t, S[h])


def attend_kernel(whole_in, whole_out, s_ref, qo_ref, qs_ref, go_ref, gs_ref, own_ref, za_ref, zc_ref, *refs):
    y_refs, (tally_ref, oo_ref, dqo_ref, swap_ref), refs = refs[:3 - 2 * whole_in], refs[3 - 2 * whole_in:7 - 2 * whole_in], refs[7 - 2 * whole_in:]
    p_refs, refs = refs[:3 - 2 * whole_out], refs[3 - 2 * whole_out:]
    loc_ref, kk, vv, kt, vt, bias, sc, pp, ds, dka, dva = refs
    core, z, y = s_ref[0], s_ref[1], s_ref[2]
    chip = 4 * z + y
    blocks = [(own_ref, (), None), (za_ref, (), chip - 4), (zc_ref, (), chip - 8)]
    for s in (1, 2, 3):
        turned = (y - s) & 3
        r, at = (y_refs[0], (turned,)) if whole_in else (y_refs[s - 1], ())
        blocks.append((r, at + (0,), 4 * z - 4 + turned))
        blocks.append((r, at + (1,), chip - s - jnp.where(y >= s, 0, 4)))
    lane = lax.broadcasted_iota(jnp.int32, (1, 128), 1)
    t_seg = jnp.concatenate([own_ref[0, 256:257], own_ref[1, 256:257]], axis=1).astype(F32)
    t_mask = jnp.concatenate([own_ref[0, 257:258], own_ref[1, 257:258]], axis=1).astype(F32)
    t_pos = jnp.concatenate([core * 128 + lane, (1 - core) * 128 + lane], axis=1)
    key = lax.broadcasted_iota(jnp.int32, (128, 256), 0)
    for b, (ref, pre, idx) in enumerate(blocks):
        for o in range(2):
            r0 = b * 256 + o * 128
            k = ref[pre + (o, slice(0, 128))]
            v = ref[pre + (o, slice(128, 256))]
            kk[r0:r0 + 128] = k
            vv[r0:r0 + 128] = v
            kt[:, r0:r0 + 128] = k.T
            vt[:, r0:r0 + 128] = v.T
            k_seg = ref[pre + (o, slice(256, 257))].astype(F32)
            n = [jnp.sum((k_seg < s).astype(F32), axis=1, keepdims=True) for s in (1, 2, 3)]
            first = jnp.where(t_seg == 3, n[2], jnp.where(t_seg == 2, n[1], jnp.where(t_seg == 1, n[0], 0.0)))
            first = first.astype(jnp.int32)
            if idx is None:
                at = core * 128 if o == 0 else (1 - core) * 128
                ok = (key >= first) & (key + at <= t_pos)
            else:
                first = jnp.where(idx >= 0, first, 128)
                ok = key >= first
            bias[r0:r0 + 128] = jnp.where(ok, 0.0, NEG)
    dka[...] = jnp.zeros_like(dka)
    dva[...] = jnp.zeros_like(dva)

    def load(h):
        cols = pl.ds(pl.multiple_of(h * 128, 128), 128)
        q = jnp.concatenate([qo_ref[:, cols], qs_ref[:, cols]], axis=0)
        g = jnp.concatenate([go_ref[:, cols], gs_ref[:, cols]], axis=0)
        return cols, q, g

    def score(t, st, b):
        rows = slice(b * 256, b * 256 + 256)
        s = mmt(kk[rows], st["q"]) + bias[rows]
        sc[t, rows] = s
        top = jnp.max(s.reshape(32, 8, 256), axis=0)
        st["top"] = top if b == 0 else jnp.maximum(st["top"], top)

    def weigh(t, st, b):
        if b == 0:
            st["top"] = jnp.max(st["top"], axis=0, keepdims=True) * CH
        rows = slice(b * 256, b * 256 + 256)
        p = jnp.exp2(sc[t, rows] * CH - st["top"])
        part = jnp.sum(p.reshape(32, 8, 256), axis=0)
        st["mass"] = part if b == 0 else st["mass"] + part
        pp[t, rows] = p.astype(BF)

    def output(t, st):
        inv = 1.0 / jnp.sum(st["mass"], axis=0, keepdims=True)
        ot = (mm(vt[...], pp[t]) * inv).astype(BF)
        out = ot.T
        oo_ref[:, st["cols"]] = out[:128]
        swap_ref[0, :, st["cols"]] = out[128:]
        st["delta"] = jnp.sum(ot.astype(F32) * st["g"].T.astype(F32), axis=0, keepdims=True)
        st["inv"] = inv * t_mask
        col = jnp.broadcast_to(st["inv"], (128, 256)).T
        st["qn"] = (st["q"].astype(F32) * col).astype(BF)
        st["gn"] = (st["g"].astype(F32) * col).astype(BF)

    def dscore(t, st, b):
        rows = slice(b * 256, b * 256 + 256)
        ds[t, rows] = (pp[t, rows].astype(F32) * (mmt(vv[rows], st["g"]) - st["delta"])).astype(BF)

    def dvalue(t, st, b):
        rows = slice(b * 256, b * 256 + 256)
        dva[rows] += mm(pp[t, rows], st["gn"])

    def dkey(t, st, b):
        rows = slice(b * 256, b * 256 + 256)
        dka[rows] += mm(ds[t, rows], st["qn"])

    def dquery(t, st):
        dq = (mm(kt[...], ds[t]) * (st["inv"] * (1.0 / math.sqrt(128)))).astype(BF).T
        dqo_ref[:, st["cols"]] = dq[:128]
        swap_ref[1, :, st["cols"]] = dq[128:]

    def start(h):
        st = {}
        st["cols"], st["q"], st["g"] = load(h)
        return st

    run_heads(score, weigh, output, dscore, dvalue, dkey, dquery, start)
    tally = tally_ref[...]
    high = jnp.floor(tally * (1 / 32))
    digits = jnp.concatenate([high, tally - 32 * high], axis=0).astype(BF)
    for b in range(NB):
        for o in range(2):
            rows = slice(b * 256 + o * 128, b * 256 + o * 128 + 128)
            if b < 3:
                loc_ref[b, o, 0:128] = dka[rows]
                loc_ref[b, o, 128:256] = dva[rows]
            else:
                s = (b - 1) // 2
                ref, at = (p_refs[0], ((y - s) & 3,)) if whole_out else (p_refs[s - 1], ())
                at = at + ((b - 3) % 2, o)
                ref[at + (slice(0, 128),)] = dka[rows].astype(BF)
                ref[at + (slice(128, 256),)] = dva[rows].astype(BF)
                ref[at + (slice(256, 272),)] = digits


def whole(a):
    return pl.BlockSpec(a.shape, lambda i, s, n=len(a.shape): (0,) * n)


def attend(scal, j, q, qs, g, gs, own, za, zc, ys, tally, whole_out):
    wide = lambda f: pl.BlockSpec((128, 1024), f)
    mine = wide(lambda i, s: (0, s[0] * 2 + j))
    other = wide(lambda i, s: (0, j))
    rows = jax.ShapeDtypeStruct((128, 1024), BF)
    pair = jax.ShapeDtypeStruct((2, 128, 1024), BF)
    part = jax.ShapeDtypeStruct((2, 2, 272, 128), BF)
    loc = jax.ShapeDtypeStruct((3, 2, 256, 128), F32)
    parts = [jax.ShapeDtypeStruct((4, 2, 2, 272, 128), BF)] if whole_out else [part] * 3
    outs = [rows, rows, pair, *parts, loc]
    n = NB * 256
    ins = (own, za, zc, *ys, tally)
    return pl.pallas_call(
        functools.partial(attend_kernel, len(ys) == 1, whole_out),
        out_shape=outs,
        grid_spec=pltpu.PrefetchScalarGridSpec(
            num_scalar_prefetch=1,
            grid=(1,),
            in_specs=[mine, other, mine, other] + [whole(a) for a in ins],
            out_specs=[whole(o) for o in outs],
            scratch_shapes=[
                pltpu.VMEM((n, 128), BF), pltpu.VMEM((n, 128), BF), pltpu.VMEM((128, n), BF), pltpu.VMEM((128, n), BF),
                pltpu.VMEM((n, 256), F32), pltpu.VMEM((2, n, 256), F32), pltpu.VMEM((2, n, 256), BF),
                pltpu.VMEM((2, n, 256), BF), pltpu.VMEM((n, 128), F32), pltpu.VMEM((n, 128), F32),
            ],
        ),
        compiler_params=pltpu.CompilerParams(vmem_limit_bytes=48 * 2**20),
        cost_estimate=pl.CostEstimate(flops=15 * 2**30, bytes_accessed=4 * 2**20, transcendentals=5 * 2**20),
        name="attend",
    )(scal, q, qs, g, gs, *ins)


def small(kernel, scal, ins, outs, name, aliases={}, passed=(), after=()):
    spot = pl.BlockSpec(memory_space=pl.ANY)
    corner = lambda a: pl.BlockSpec((1,) * (len(a.shape) - 2) + (16, 128), lambda i, s, n=len(a.shape): (0,) * n)
    kept = len(outs) - len(aliases)
    return pl.pallas_call(
        kernel,
        out_shape=outs,
        grid_spec=pltpu.PrefetchScalarGridSpec(
            num_scalar_prefetch=1,
            grid=(1,),
            in_specs=[whole(a) for a in ins] + [spot] * len(passed) + [corner(a) for a in after],
            out_specs=[whole(o) for o in outs[:kept]] + [spot] * len(aliases),
        ),
        input_output_aliases={1 + len(ins) + a: kept + b for a, b in aliases.items()},
        compiler_params=pltpu.CompilerParams(vmem_limit_bytes=32 * 2**20),
        name=name,
    )(scal, *ins, *passed, *after)


def spread_all_kernel(s_ref, own_ref, za_ref, zc_ref, out_ref):
    y = s_ref[2]
    for t in range(4):
        out_ref[t, 0] = za_ref[...]

        @pl.when(y < t)
        def _():
            out_ref[t, 1] = own_ref[...]

        @pl.when(y >= t)
        def _():
            out_ref[t, 1] = zc_ref[...]


def spread_three_kernel(s_ref, own_ref, za_ref, zc_ref, _, *out_refs):
    y = s_ref[2]
    for s, out_ref in zip((1, 2, 3), out_refs):
        out_ref[0] = za_ref[...]

        @pl.when(y + s < 4)
        def _():
            out_ref[1] = own_ref[...]

        @pl.when(y + s >= 4)
        def _():
            out_ref[1] = zc_ref[...]


def sum_kernel(whole_in, s_ref, *refs):
    y = s_ref[2]
    got = refs[:1] if whole_in else refs[:3]
    loc_ref, tally_ref, back_a, back_c, here, total = refs[len(got):len(got) + 6] if whole_in else refs[3:5] + refs[6:10]
    a, c, h, tally = loc_ref[1], loc_ref[2], loc_ref[0], tally_ref[...]
    for s in (1, 2, 3):
        r, at = (got[0], ((y + s) & 3,)) if whole_in else (got[s - 1], ())
        a = a + r[at + (0, slice(None), slice(0, 256))].astype(F32)
        b = r[at + (1, slice(None), slice(0, 256))].astype(F32)
        h = h + jnp.where(y + s < 4, b, 0.0)
        c = c + jnp.where(y + s < 4, 0.0, b)
        d = r[at + (0, 0, slice(256, 272))].astype(F32)
        tally = tally + 32.0 * d[:8] + d[8:]
    back_a[...] = a.astype(BF)
    back_c[...] = c.astype(BF)
    here[...] = h
    total[...] = tally


def final_kernel(s_ref, h0, a0, c0, h1, a1, c1, tally_ref, _, mine, theirs):
    scale = (4.0 * 4096) / tally_ref[0:1]
    for j, (h, a, c) in enumerate(((h0, a0, c0), (h1, a1, c1))):
        for o, out in enumerate((mine, theirs)):
            t = (h[o] + a[o].astype(F32) + c[o].astype(F32)) * scale
            out[j, 0:128] = (t[0:128] * (1.0 / math.sqrt(128))).astype(BF)
            out[j, 128:256] = t[128:256].astype(BF)


def place_kernel(s_ref, mine, theirs, dk_ref, dv_ref):
    core = s_ref[0]
    for c, src in ((core, mine), (1 - core, theirs)):
        for j in range(2):
            cols = pl.ds(pl.multiple_of(c * 256 + j * 128, 128), 128)
            dk_ref[:, cols] = src[j, 0:128]
            dv_ref[:, cols] = src[j, 128:256]


def rows_kernel(s_ref, oo0, oo1, dq0, dq1, r0, r1, tally_ref, out_ref, dq_ref):
    core = s_ref[0]
    scale = (4.0 * 4096) / tally_ref[0:1, 0:1]
    for j, (o, d, r) in enumerate(((oo0, dq0, r0), (oo1, dq1, r1))):
        mine = pl.ds(pl.multiple_of(core * 2048 + j * 1024, 128), 1024)
        theirs = pl.ds(pl.multiple_of((1 - core) * 2048 + j * 1024, 128), 1024)
        out_ref[:, mine] = o[...]
        out_ref[:, theirs] = r[0]
        dq_ref[:, mine] = (d[...].astype(F32) * scale).astype(BF)
        dq_ref[:, theirs] = (r[1].astype(F32) * scale).astype(BF)


def shard(queries, keys, values, out_grad, segment_ids, loss_mask):
    me = lax.axis_index("ctx")
    core, y, z = me & 1, (me >> 1) & 3, me >> 3
    q, k, v, g = queries[0], keys[0], values[0], out_grad[0]

    def send(x, target, turn=False):
        pairs = []
        for i in range(32):
            zz, yy, cc = target(i // 8, i // 2 % 4, i % 2)
            if turn or 0 <= zz < 4:
                pairs.append((i, (zz % 4 * 4 + yy % 4) * 2 + cc % 2))
        return lax.ppermute(x, "ctx", pairs)

    swap = lambda x: send(x, lambda z, y, c: (z, y, c + 1))
    along_z = lambda x, a, turn=False: send(x, lambda z, y, c: (z + a, y, c), turn)
    along_y = lambda x, s: send(x, lambda z, y, c: (z, y + s, c))
    rows_of_y = [[(zz * 4 + yy) * 2 + cc for yy in range(4)] for zz in range(4) for cc in range(2)]
    trade_y = lambda x: lax.all_to_all(x, "ctx", 0, 0, axis_index_groups=rows_of_y)

    info = jnp.concatenate([segment_ids.astype(BF), loss_mask.astype(BF), jnp.zeros((14, 128), BF)], axis=0)

    def payload(c):
        heads = lambda a: lax.dynamic_slice(a, (0, c * 256), (128, 256)).reshape(128, 2, 128).transpose(1, 0, 2)
        return jnp.concatenate([heads(k), heads(v), jnp.broadcast_to(info, (2, 16, 128))], axis=1)

    own = jnp.stack([payload(core), swap(payload(1 - core))], axis=1)
    half = lambda a: lax.dynamic_slice(a, (0, (1 - core) * 2048), (128, 2048))
    qs, gs = swap(half(q)), swap(half(g))
    za, zc = zip(*[(along_z(own[j], 1, True), along_z(own[j], 2)) for j in range(2)])
    scal = jnp.stack([core, z, y]).astype(jnp.int32)

    counted = jnp.broadcast_to(jnp.sum(za[0][:, 257].astype(F32)), (8, 128))
    for step in (1, 2):
        counted = counted + lax.ppermute(counted, "dp", [(i, i ^ step) for i in range(4)])

    kind = jax.ShapeDtypeStruct
    block = kind((2, 2, 272, 128), BF)
    y_all = trade_y(small(spread_all_kernel, scal, (own[0], za[0], zc[0]), [kind((4, 2, 2, 272, 128), BF)], "spread_all")[0])
    three = small(spread_three_kernel, scal, (own[1], za[1], zc[1]), [block] * 3, "spread_three", after=(y_all,))
    ys = [(y_all,), [along_y(x, s) for s, x in zip((1, 2, 3), three)]]

    oo0, dq0, pair0, *parts, loc0 = attend(scal, 0, q, qs, g, gs, own[0], za[0], zc[0], ys[0], counted, False)
    got0 = [along_y(p, -s) for s, p in zip((1, 2, 3), parts)]
    oo1, dq1, pair1, part1, loc1 = attend(scal, 1, q, qs, g, gs, own[1], za[1], zc[1], ys[1], counted, True)
    sums = [kind((2, 256, 128), BF)] * 2 + [kind((2, 256, 128), F32), kind((8, 128), F32)]
    back_a0, back_c0, here0, tally, part1 = small(
        functools.partial(sum_kernel, False), scal, (*got0, loc0, counted), sums + [part1], "sum_first", {0: 0}, (part1,)
    )
    a0, c0 = along_z(back_a0, -1), along_z(back_c0, -2)
    r0, r1 = swap(pair0), swap(pair1)
    tally = tally + send(tally, lambda z, y, c: (z ^ 1, y, c))
    back_a1, back_c1, here1, _ = small(
        functools.partial(sum_kernel, True), scal, (trade_y(part1), loc1, counted), sums, "sum_second"
    )
    a1, c1 = along_z(back_a1, -1), along_z(back_c1, -2)
    tally = tally + send(tally, lambda z, y, c: (z ^ 2, y, c))
    wide = kind((128, 4096), BF)
    attn, dq = small(rows_kernel, scal, (oo0, oo1, dq0, dq1, r0, r1, tally), [wide] * 2, "rows")
    sides = kind((2, 256, 128), BF)
    mine, theirs = small(final_kernel, scal, (here0, a0, c0, here1, a1, c1, tally), [sides] * 2, "final", after=(dq,))
    dk, dv = small(place_kernel, scal, (mine, swap(theirs)), [kind((128, 512), BF)] * 2, "place")
    return attn[None], dq[None], dk[None], dv[None]


def solution(mesh):
    rows, ids = P("dp", "ctx", None), P("dp", "ctx")
    return jax.shard_map(
        shard, mesh=mesh, in_specs=(rows,) * 4 + (ids,) * 2, out_specs=(rows,) * 4, check_vma=False
    )
```

```python
import math, functools
import jax, jax.numpy as jnp
from jax import lax
from jax.sharding import PartitionSpec as P
from jax.experimental import pallas as pl
from jax.experimental.pallas import tpu as pltpu

NEG = -1e30
CH = math.log2(math.e) / math.sqrt(128)
BF, F32 = jnp.bfloat16, jnp.float32
NB = 9
NT = (((1,), (1,)), ((), ()))


def mm(a, b):
    return jnp.dot(a, b, preferred_element_type=F32)


def mmt(a, b):
    return lax.dot_general(a, b, NT, preferred_element_type=F32)


def run_heads(score, weigh, output, dscore, dvalue, dkey, dquery, start):
    R = range(NB)

    def pair(i, _):
        S = [start(2 * i), start(2 * i + 1)]
        for t in (0, 1):
            for b in R:
                score(t, S[t], b)
        for t in (0, 1):
            for b in R:
                weigh(t, S[t], b)
        for t in (0, 1):
            output(t, S[t])
        for t in (0, 1):
            for b in R:
                dscore(t, S[t], b)
        for t in (0, 1):
            for b in R:
                dvalue(t, S[t], b)
        for t in (0, 1):
            for b in R:
                dkey(t, S[t], b)
        for t in (0, 1):
            dquery(t, S[t])
        return 0

    lax.fori_loop(0, 4, pair, 0)


def attend_kernel(s_ref, qo_ref, qs_ref, go_ref, gs_ref, own_ref, za_ref, zc_ref, y_ref, tally_ref,
                  oo_ref, dqo_ref, swap_ref, p_ref, loc_ref, kk, vv, kt, vt, bias, sc, pp, ds, dka, dva):
    core, z, y = s_ref[0], s_ref[1], s_ref[2]
    chip = 4 * z + y
    blocks = [(own_ref, (), None), (za_ref, (), chip - 4), (zc_ref, (), chip - 8)]
    for s in (1, 2, 3):
        turned = (y - s) & 3
        blocks.append((y_ref, (turned, 0), 4 * z - 4 + turned))
        blocks.append((y_ref, (turned, 1), chip - s - jnp.where(y >= s, 0, 4)))
    lane = lax.broadcasted_iota(jnp.int32, (1, 128), 1)
    t_seg = jnp.concatenate([own_ref[0, 256:257], own_ref[1, 256:257]], axis=1).astype(F32)
    t_mask = jnp.concatenate([own_ref[0, 257:258], own_ref[1, 257:258]], axis=1).astype(F32)
    t_pos = jnp.concatenate([core * 128 + lane, (1 - core) * 128 + lane], axis=1)
    key = lax.broadcasted_iota(jnp.int32, (128, 256), 0)
    for b, (ref, pre, idx) in enumerate(blocks):
        for o in range(2):
            r0 = b * 256 + o * 128
            k = ref[pre + (o, slice(0, 128))]
            v = ref[pre + (o, slice(128, 256))]
            kk[r0:r0 + 128] = k
            vv[r0:r0 + 128] = v
            kt[:, r0:r0 + 128] = k.T
            vt[:, r0:r0 + 128] = v.T
            k_seg = ref[pre + (o, slice(256, 257))].astype(F32)
            n = [jnp.sum((k_seg < s).astype(F32), axis=1, keepdims=True) for s in (1, 2, 3)]
            first = jnp.where(t_seg == 3, n[2], jnp.where(t_seg == 2, n[1], jnp.where(t_seg == 1, n[0], 0.0)))
            first = first.astype(jnp.int32)
            if idx is None:
                at = core * 128 if o == 0 else (1 - core) * 128
                ok = (key >= first) & (key + at <= t_pos)
            else:
                first = jnp.where(idx >= 0, first, 128)
                ok = key >= first
            bias[r0:r0 + 128] = jnp.where(ok, 0.0, NEG)
    dka[...] = jnp.zeros_like(dka)
    dva[...] = jnp.zeros_like(dva)

    def load(h):
        cols = pl.ds(pl.multiple_of(h * 128, 128), 128)
        q = jnp.concatenate([qo_ref[:, cols], qs_ref[:, cols]], axis=0)
        g = jnp.concatenate([go_ref[:, cols], gs_ref[:, cols]], axis=0)
        return cols, q, g

    def score(t, st, b):
        rows = slice(b * 256, b * 256 + 256)
        s = mmt(kk[rows], st["q"]) + bias[rows]
        sc[t, rows] = s
        top = jnp.max(s.reshape(32, 8, 256), axis=0)
        st["top"] = top if b == 0 else jnp.maximum(st["top"], top)

    def weigh(t, st, b):
        if b == 0:
            st["top"] = jnp.max(st["top"], axis=0, keepdims=True) * CH
        rows = slice(b * 256, b * 256 + 256)
        p = jnp.exp2(sc[t, rows] * CH - st["top"])
        part = jnp.sum(p.reshape(32, 8, 256), axis=0)
        st["mass"] = part if b == 0 else st["mass"] + part
        pp[t, rows] = p.astype(BF)

    def output(t, st):
        inv = 1.0 / jnp.sum(st["mass"], axis=0, keepdims=True)
        ot = (mm(vt[...], pp[t]) * inv).astype(BF)
        out = ot.T
        oo_ref[:, st["cols"]] = out[:128]
        swap_ref[0, :, st["cols"]] = out[128:]
        st["delta"] = jnp.sum(ot.astype(F32) * st["g"].T.astype(F32), axis=0, keepdims=True)
        st["inv"] = inv * t_mask
        col = jnp.broadcast_to(st["inv"], (128, 256)).T
        st["qn"] = (st["q"].astype(F32) * col).astype(BF)
        st["gn"] = (st["g"].astype(F32) * col).astype(BF)

    def dscore(t, st, b):
        rows = slice(b * 256, b * 256 + 256)
        ds[t, rows] = (pp[t, rows].astype(F32) * (mmt(vv[rows], st["g"]) - st["delta"])).astype(BF)

    def dvalue(t, st, b):
        rows = slice(b * 256, b * 256 + 256)
        dva[rows] += mm(pp[t, rows], st["gn"])

    def dkey(t, st, b):
        rows = slice(b * 256, b * 256 + 256)
        dka[rows] += mm(ds[t, rows], st["qn"])

    def dquery(t, st):
        dq = (mm(kt[...], ds[t]) * (st["inv"] * (1.0 / math.sqrt(128)))).astype(BF).T
        dqo_ref[:, st["cols"]] = dq[:128]
        swap_ref[1, :, st["cols"]] = dq[128:]

    def start(h):
        st = {}
        st["cols"], st["q"], st["g"] = load(h)
        return st

    run_heads(score, weigh, output, dscore, dvalue, dkey, dquery, start)
    tally = tally_ref[...]
    high = jnp.floor(tally * (1 / 32))
    digits = jnp.concatenate([high, tally - 32 * high], axis=0).astype(BF)
    for b in range(NB):
        for o in range(2):
            rows = slice(b * 256 + o * 128, b * 256 + o * 128 + 128)
            if b < 3:
                loc_ref[b, o, 0:128] = dka[rows]
                loc_ref[b, o, 128:256] = dva[rows]
            else:
                turned = (y - (b - 1) // 2) & 3
                p_ref[turned, (b - 3) % 2, o, 0:128] = dka[rows].astype(BF)
                p_ref[turned, (b - 3) % 2, o, 128:256] = dva[rows].astype(BF)
                p_ref[turned, (b - 3) % 2, o, 256:272] = digits


def whole(a):
    return pl.BlockSpec(a.shape, lambda i, s, n=len(a.shape): (0,) * n)


def of_head(j):
    return pl.BlockSpec((None, 2, 272, 128), lambda i, s: (j, 0, 0, 0))


def attend(scal, j, q, qs, g, gs, own, za, zc, ys, tally):
    wide = lambda f: pl.BlockSpec((128, 1024), f)
    mine = wide(lambda i, s: (0, s[0] * 2 + j))
    other = wide(lambda i, s: (0, j))
    rows = jax.ShapeDtypeStruct((128, 1024), BF)
    pair = jax.ShapeDtypeStruct((2, 128, 1024), BF)
    loc = jax.ShapeDtypeStruct((3, 2, 256, 128), F32)
    outs = [rows, rows, pair, jax.ShapeDtypeStruct((4, 2, 2, 272, 128), BF), loc]
    n = NB * 256
    ins = (own, za, zc, ys, tally)
    return pl.pallas_call(
        attend_kernel,
        out_shape=outs,
        grid_spec=pltpu.PrefetchScalarGridSpec(
            num_scalar_prefetch=1,
            grid=(1,),
            in_specs=[mine, other, mine, other] + [of_head(j)] * 3 + [whole(ys), whole(tally)],
            out_specs=[whole(o) for o in outs],
            scratch_shapes=[
                pltpu.VMEM((n, 128), BF), pltpu.VMEM((n, 128), BF), pltpu.VMEM((128, n), BF), pltpu.VMEM((128, n), BF),
                pltpu.VMEM((n, 256), F32), pltpu.VMEM((2, n, 256), F32), pltpu.VMEM((2, n, 256), BF),
                pltpu.VMEM((2, n, 256), BF), pltpu.VMEM((n, 128), F32), pltpu.VMEM((n, 128), F32),
            ],
        ),
        compiler_params=pltpu.CompilerParams(vmem_limit_bytes=60 * 2**20),
        cost_estimate=pl.CostEstimate(flops=15 * 2**30, bytes_accessed=4 * 2**20, transcendentals=5 * 2**20),
        name="attend",
    )(scal, q, qs, g, gs, *ins)


def small(kernel, scal, ins, outs, name, head=None):
    return pl.pallas_call(
        kernel,
        out_shape=outs,
        grid_spec=pltpu.PrefetchScalarGridSpec(
            num_scalar_prefetch=1,
            grid=(1,),
            in_specs=[whole(a) if head is None else of_head(head) for a in ins],
            out_specs=[whole(o) for o in outs],
        ),
        compiler_params=pltpu.CompilerParams(vmem_limit_bytes=60 * 2**20),
        name=name,
    )(scal, *ins)


def spread_kernel(s_ref, own_ref, za_ref, zc_ref, out_ref):
    y = s_ref[2]
    for t in range(4):
        out_ref[t, 0] = za_ref[...]

        @pl.when(y < t)
        def _():
            out_ref[t, 1] = own_ref[...]

        @pl.when(y >= t)
        def _():
            out_ref[t, 1] = zc_ref[...]


def sum_kernel(s_ref, got, loc_ref, tally_ref, a_mine, a_theirs, c_mine, c_theirs, here, here_theirs, total):
    y = s_ref[2]
    a, c, h, tally = loc_ref[1], loc_ref[2], loc_ref[0], tally_ref[...]
    for s in (1, 2, 3):
        t = (y + s) & 3
        a = a + got[t, 0, :, 0:256].astype(F32)
        b = got[t, 1, :, 0:256].astype(F32)
        h = h + jnp.where(y + s < 4, b, 0.0)
        c = c + jnp.where(y + s < 4, 0.0, b)
        d = got[t, 0, 0, 256:272].astype(F32)
        tally = tally + 32.0 * d[:8] + d[8:]
    a_mine[...] = a[0].astype(BF)
    a_theirs[...] = a[1].astype(BF)
    c_mine[...] = c[0].astype(BF)
    c_theirs[...] = c[1].astype(BF)
    here[...] = h[0]
    here_theirs[...] = h[1].astype(BF)
    if total is not None:
        total[...] = tally


def sum_both_kernel(s_ref, got, loc_ref, tally_ref, *refs):
    olds, news = refs[:6], refs[6:12]
    for old, new in zip(olds, news):
        new[0] = old[...]
    sum_kernel(s_ref, got, loc_ref, tally_ref, *[new.at[1] for new in news], None)


def final_kernel(s_ref, tally_ref, *refs):
    core = s_ref[0]
    dk_ref, dv_ref = refs[6:]
    scale = (4.0 * 4096) / tally_ref[0:1]
    for j in range(2):
        for c, three in ((core, refs[:3]), (1 - core, refs[3:6])):
            t = sum(r[j].astype(F32) for r in three) * scale
            cols = pl.ds(pl.multiple_of(c * 256 + j * 128, 128), 128)
            dk_ref[:, cols] = (t[0:128] * (1.0 / math.sqrt(128))).astype(BF)
            dv_ref[:, cols] = t[128:256].astype(BF)


def rows_kernel(s_ref, oo0, oo1, dq0, dq1, r0, r1, tally_ref, out_ref, dq_ref):
    core = s_ref[0]
    scale = (4.0 * 4096) / tally_ref[0:1, 0:1]
    for j, (o, d, r) in enumerate(((oo0, dq0, r0), (oo1, dq1, r1))):
        mine = pl.ds(pl.multiple_of(core * 2048 + j * 1024, 128), 1024)
        theirs = pl.ds(pl.multiple_of((1 - core) * 2048 + j * 1024, 128), 1024)
        out_ref[:, mine] = o[...]
        out_ref[:, theirs] = r[0]
        dq_ref[:, mine] = (d[...].astype(F32) * scale).astype(BF)
        dq_ref[:, theirs] = (r[1].astype(F32) * scale).astype(BF)


def shard(queries, keys, values, out_grad, segment_ids, loss_mask):
    me = lax.axis_index("ctx")
    core, y, z = me & 1, (me >> 1) & 3, me >> 3
    q, k, v, g = queries[0], keys[0], values[0], out_grad[0]

    def send(x, target, turn=False):
        pairs = []
        for i in range(32):
            zz, yy, cc = target(i // 8, i // 2 % 4, i % 2)
            if turn or 0 <= zz < 4:
                pairs.append((i, (zz % 4 * 4 + yy % 4) * 2 + cc % 2))
        return lax.ppermute(x, "ctx", pairs)

    swap = lambda x: send(x, lambda z, y, c: (z, y, c + 1))
    along_z = lambda x, a, turn=False: send(x, lambda z, y, c: (z + a, y, c), turn)
    rows_of_y = [[(zz * 4 + yy) * 2 + cc for yy in range(4)] for zz in range(4) for cc in range(2)]
    trade_y = lambda x: lax.all_to_all(x, "ctx", 0, 0, axis_index_groups=rows_of_y)

    info = jnp.concatenate([segment_ids.astype(BF), loss_mask.astype(BF), jnp.zeros((14, 128), BF)], axis=0)

    def payload(c):
        heads = lambda a: lax.dynamic_slice(a, (0, c * 256), (128, 256)).reshape(128, 2, 128).transpose(1, 0, 2)
        return jnp.concatenate([heads(k), heads(v), jnp.broadcast_to(info, (2, 16, 128))], axis=1)

    own = jnp.stack([payload(core), swap(payload(1 - core))], axis=1)
    half = lambda a: lax.dynamic_slice(a, (0, (1 - core) * 2048), (128, 2048))
    qs, gs = swap(half(q)), swap(half(g))
    za, zc = along_z(own, 1, True), along_z(own, 2)
    scal = jnp.stack([core, z, y]).astype(jnp.int32)

    counted = jnp.broadcast_to(jnp.sum(za[0][:, 257].astype(F32)), (8, 128))
    for step in (1, 2):
        counted = counted + lax.ppermute(counted, "dp", [(i, i ^ step) for i in range(4)])

    kind = jax.ShapeDtypeStruct
    four = kind((4, 2, 2, 272, 128), BF)
    ys = [trade_y(small(spread_kernel, scal, (own, za, zc), [four], "spread", head=j)[0]) for j in range(2)]

    side, side32 = kind((256, 128), BF), kind((256, 128), F32)
    sums = [side] * 4 + [side32, side, kind((8, 128), F32)]
    to = lambda x, a, c: send(x, lambda z, yy, cc: (z + a, yy, cc + c))
    oo0, dq0, pair0, part0, loc0 = attend(scal, 0, q, qs, g, gs, own, za, zc, ys[0], counted)
    got0 = trade_y(part0)
    oo1, dq1, pair1, part1, loc1 = attend(scal, 1, q, qs, g, gs, own, za, zc, ys[1], counted)
    first = small(sum_kernel, scal, (got0, loc0, counted), sums, "sum_first")
    tally = first[-1]
    sides, sides32 = kind((2, 256, 128), BF), kind((2, 256, 128), F32)
    a_mine, a_theirs, c_mine, c_theirs, here, here_theirs = small(
        sum_both_kernel, scal, (trade_y(part1), loc1, counted, *first[:-1]), [sides] * 4 + [sides32, sides], "sum_both"
    )
    kv = (here, to(a_mine, -1, 0), to(c_mine, -2, 0), swap(here_theirs), to(a_theirs, -1, 1), to(c_theirs, -2, 1))
    for step in (1, 2):
        tally = tally + send(tally, lambda z, y, c: (z ^ step, y, c))
    wide = kind((128, 4096), BF)
    attn, dq = small(rows_kernel, scal, (oo0, oo1, dq0, dq1, swap(pair0), swap(pair1), tally), [wide] * 2, "rows")
    dk, dv = small(final_kernel, scal, (tally, *kv), [kind((128, 512), BF)] * 2, "final")
    return attn[None], dq[None], dk[None], dv[None]


def solution(mesh):
    rows, ids = P("dp", "ctx", None), P("dp", "ctx")
    return jax.shard_map(
        shard, mesh=mesh, in_specs=(rows,) * 4 + (ids,) * 2, out_specs=(rows,) * 4, check_vma=False
    )
```

```python
import math, functools
import jax, jax.numpy as jnp
from jax import lax
from jax.sharding import PartitionSpec as P
from jax.experimental import pallas as pl
from jax.experimental.pallas import tpu as pltpu

NEG = -1e30
CH = math.log2(math.e) / math.sqrt(128)
BF, F32 = jnp.bfloat16, jnp.float32
NB = 9
NT = (((1,), (1,)), ((), ()))


def mm(a, b):
    return jnp.dot(a, b, preferred_element_type=F32)


def mmt(a, b):
    return lax.dot_general(a, b, NT, preferred_element_type=F32)


def run_heads(score, weigh, output, dscore, dvalue, dkey, dquery, start):
    R = range(NB)

    def pair(i, _):
        S = [start(2 * i), start(2 * i + 1)]
        for t in (0, 1):
            for b in R:
                score(t, S[t], b)
        for t in (0, 1):
            for b in R:
                weigh(t, S[t], b)
        for t in (0, 1):
            output(t, S[t])
        for t in (0, 1):
            for b in R:
                dscore(t, S[t], b)
        for t in (0, 1):
            for b in R:
                dvalue(t, S[t], b)
        for t in (0, 1):
            for b in R:
                dkey(t, S[t], b)
        for t in (0, 1):
            dquery(t, S[t])
        return 0

    lax.fori_loop(0, 4, pair, 0)


def attend_kernel(s_ref, qo_ref, qs_ref, go_ref, gs_ref, own_ref, za_ref, zc_ref, y_ref, tally_ref,
                  oo_ref, dqo_ref, swap_ref, p_ref, loc_ref, cnt_ref, kk, vv, kt, vt, bias, sc, pp, ds, dka, dva):
    core, z, y = s_ref[0], s_ref[1], s_ref[2]
    chip = 4 * z + y
    blocks = [(own_ref, (), None), (za_ref, (), chip - 4), (zc_ref, (), chip - 8)]
    for s in (1, 2, 3):
        turned = (y - s) & 3
        blocks.append((y_ref, (turned, 0), 4 * z - 4 + turned))
        blocks.append((y_ref, (turned, 1), chip - s - jnp.where(y >= s, 0, 4)))
    lane = lax.broadcasted_iota(jnp.int32, (1, 128), 1)
    t_seg = jnp.concatenate([own_ref[0, 256:257], own_ref[1, 256:257]], axis=1).astype(F32)
    t_mask = jnp.concatenate([own_ref[0, 257:258], own_ref[1, 257:258]], axis=1).astype(F32)
    t_pos = jnp.concatenate([core * 128 + lane, (1 - core) * 128 + lane], axis=1)
    key = lax.broadcasted_iota(jnp.int32, (128, 256), 0)
    for b, (ref, pre, idx) in enumerate(blocks):
        for o in range(2):
            r0 = b * 256 + o * 128
            k = ref[pre + (o, slice(0, 128))]
            v = ref[pre + (o, slice(128, 256))]
            kk[r0:r0 + 128] = k
            vv[r0:r0 + 128] = v
            kt[:, r0:r0 + 128] = k.T
            vt[:, r0:r0 + 128] = v.T
            k_seg = ref[pre + (o, slice(256, 257))].astype(F32)
            n = [jnp.sum((k_seg < s).astype(F32), axis=1, keepdims=True) for s in (1, 2, 3)]
            first = jnp.where(t_seg == 3, n[2], jnp.where(t_seg == 2, n[1], jnp.where(t_seg == 1, n[0], 0.0)))
            first = first.astype(jnp.int32)
            if idx is None:
                at = core * 128 if o == 0 else (1 - core) * 128
                ok = (key >= first) & (key + at <= t_pos)
            else:
                first = jnp.where(idx >= 0, first, 128)
                ok = key >= first
            bias[r0:r0 + 128] = jnp.where(ok, 0.0, NEG)
    dka[...] = jnp.zeros_like(dka)
    dva[...] = jnp.zeros_like(dva)

    def load(h):
        cols = pl.ds(pl.multiple_of(h * 128, 128), 128)
        q = jnp.concatenate([qo_ref[:, cols], qs_ref[:, cols]], axis=0)
        g = jnp.concatenate([go_ref[:, cols], gs_ref[:, cols]], axis=0)
        return cols, q, g

    def score(t, st, b):
        rows = slice(b * 256, b * 256 + 256)
        s = mmt(kk[rows], st["q"]) + bias[rows]
        sc[t, rows] = s
        top = jnp.max(s.reshape(32, 8, 256), axis=0)
        st["top"] = top if b == 0 else jnp.maximum(st["top"], top)

    def weigh(t, st, b):
        if b == 0:
            st["top"] = jnp.max(st["top"], axis=0, keepdims=True) * CH
        rows = slice(b * 256, b * 256 + 256)
        p = jnp.exp2(sc[t, rows] * CH - st["top"])
        part = jnp.sum(p.reshape(32, 8, 256), axis=0)
        st["mass"] = part if b == 0 else st["mass"] + part
        pp[t, rows] = p.astype(BF)

    def output(t, st):
        inv = 1.0 / jnp.sum(st["mass"], axis=0, keepdims=True)
        ot = (mm(vt[...], pp[t]) * inv).astype(BF)
        out = ot.T
        oo_ref[:, st["cols"]] = out[:128]
        swap_ref[0, :, st["cols"]] = out[128:]
        st["delta"] = jnp.sum(ot.astype(F32) * st["g"].T.astype(F32), axis=0, keepdims=True)
        st["inv"] = inv * t_mask
        col = jnp.broadcast_to(st["inv"], (128, 256)).T
        st["qn"] = (st["q"].astype(F32) * col).astype(BF)
        st["gn"] = (st["g"].astype(F32) * col).astype(BF)

    def dscore(t, st, b):
        rows = slice(b * 256, b * 256 + 256)
        ds[t, rows] = (pp[t, rows].astype(F32) * (mmt(vv[rows], st["g"]) - st["delta"])).astype(BF)

    def dvalue(t, st, b):
        rows = slice(b * 256, b * 256 + 256)
        dva[rows] += mm(pp[t, rows], st["gn"])

    def dkey(t, st, b):
        rows = slice(b * 256, b * 256 + 256)
        dka[rows] += mm(ds[t, rows], st["qn"])

    def dquery(t, st):
        dq = (mm(kt[...], ds[t]) * (st["inv"] * (1.0 / math.sqrt(128)))).astype(BF).T
        dqo_ref[:, st["cols"]] = dq[:128]
        swap_ref[1, :, st["cols"]] = dq[128:]

    def start(h):
        st = {}
        st["cols"], st["q"], st["g"] = load(h)
        return st

    run_heads(score, weigh, output, dscore, dvalue, dkey, dquery, start)
    tally = tally_ref[...]
    for s in (1, 2, 3):
        digits = y_ref[(y - s) & 3, 0, 0, 256:272].astype(F32)
        tally = tally + 32.0 * digits[2:3] + digits[3:4]
    cnt_ref[...] = tally
    for b in range(NB):
        for o in range(2):
            rows = slice(b * 256 + o * 128, b * 256 + o * 128 + 128)
            if b < 3:
                loc_ref[b, o, 0:128] = dka[rows]
                loc_ref[b, o, 128:256] = dva[rows]
            else:
                turned = (y - (b - 1) // 2) & 3
                p_ref[turned, (b - 3) % 2, o, 0:128] = dka[rows].astype(BF)
                p_ref[turned, (b - 3) % 2, o, 128:256] = dva[rows].astype(BF)


def whole(a):
    return pl.BlockSpec(a.shape, lambda i, s, n=len(a.shape): (0,) * n)


def of_head(j):
    return pl.BlockSpec((None, 2, 272, 128), lambda i, s: (j, 0, 0, 0))


def attend(scal, j, q, qs, g, gs, own, za, zc, ys, tally):
    wide = lambda f: pl.BlockSpec((128, 1024), f)
    mine = wide(lambda i, s: (0, s[0] * 2 + j))
    other = wide(lambda i, s: (0, j))
    rows = jax.ShapeDtypeStruct((128, 1024), BF)
    pair = jax.ShapeDtypeStruct((2, 128, 1024), BF)
    loc = jax.ShapeDtypeStruct((3, 2, 256, 128), F32)
    outs = [rows, rows, pair, jax.ShapeDtypeStruct((4, 2, 2, 256, 128), BF), loc, jax.ShapeDtypeStruct((8, 128), F32)]
    n = NB * 256
    ins = (own, za, zc, ys, tally)
    return pl.pallas_call(
        attend_kernel,
        out_shape=outs,
        grid_spec=pltpu.PrefetchScalarGridSpec(
            num_scalar_prefetch=1,
            grid=(1,),
            in_specs=[mine, other, mine, other] + [of_head(j)] * 3 + [whole(ys), whole(tally)],
            out_specs=[whole(o) for o in outs],
            scratch_shapes=[
                pltpu.VMEM((n, 128), BF), pltpu.VMEM((n, 128), BF), pltpu.VMEM((128, n), BF), pltpu.VMEM((128, n), BF),
                pltpu.VMEM((n, 256), F32), pltpu.VMEM((2, n, 256), F32), pltpu.VMEM((2, n, 256), BF),
                pltpu.VMEM((2, n, 256), BF), pltpu.VMEM((n, 128), F32), pltpu.VMEM((n, 128), F32),
            ],
        ),
        compiler_params=pltpu.CompilerParams(vmem_limit_bytes=60 * 2**20),
        cost_estimate=pl.CostEstimate(flops=15 * 2**30, bytes_accessed=4 * 2**20, transcendentals=5 * 2**20),
        name="attend",
    )(scal, q, qs, g, gs, *ins)


def small(kernel, scal, ins, outs, name, head=None):
    return pl.pallas_call(
        kernel,
        out_shape=outs,
        grid_spec=pltpu.PrefetchScalarGridSpec(
            num_scalar_prefetch=1,
            grid=(1,),
            in_specs=[of_head(head) if len(a.shape) == 4 and head is not None else whole(a) for a in ins],
            out_specs=[whole(o) for o in outs],
        ),
        compiler_params=pltpu.CompilerParams(vmem_limit_bytes=16 * 2**20),
        name=name,
    )(scal, *ins)


def spread_kernel(s_ref, own_ref, za_ref, zc_ref, tally_ref, out_ref):
    y = s_ref[2]
    tally = tally_ref[...]
    high = jnp.floor(tally * (1 / 32))
    row = lax.broadcasted_iota(jnp.int32, (16, 128), 0)
    info = za_ref[0, 256:272].astype(F32)
    info = jnp.where(row == 2, high[:1], jnp.where(row == 3, (tally - 32 * high)[:1], info)).astype(BF)
    for t in range(4):
        out_ref[t, 0] = za_ref[...]
        out_ref[t, 0, 0, 256:272] = info

        @pl.when(y < t)
        def _():
            out_ref[t, 1] = own_ref[...]

        @pl.when(y >= t)
        def _():
            out_ref[t, 1] = zc_ref[...]


def sum_kernel(s_ref, got0, loc0, got1, loc1, a_mine, a_theirs, c_mine, c_theirs, here, here_theirs):
    y = s_ref[2]
    for j, (got, loc_ref) in enumerate(((got0, loc0), (got1, loc1))):
        a, c, h = loc_ref[1], loc_ref[2], loc_ref[0]
        for s in (1, 2, 3):
            t = (y + s) & 3
            a = a + got[t, 0].astype(F32)
            b = got[t, 1].astype(F32)
            h = h + jnp.where(y + s < 4, b, 0.0)
            c = c + jnp.where(y + s < 4, 0.0, b)
        a_mine[j] = a[0].astype(BF)
        a_theirs[j] = a[1].astype(BF)
        c_mine[j] = c[0].astype(BF)
        c_theirs[j] = c[1].astype(BF)
        here[j] = h[0]
        here_theirs[j] = h[1].astype(BF)


def final_kernel(s_ref, tally_ref, *refs):
    core = s_ref[0]
    dk_ref, dv_ref = refs[6:]
    scale = (4.0 * 4096) / tally_ref[0:1]
    for j in range(2):
        for c, three in ((core, refs[:3]), (1 - core, refs[3:6])):
            t = sum(r[j].astype(F32) for r in three) * scale
            cols = pl.ds(pl.multiple_of(c * 256 + j * 128, 128), 128)
            dk_ref[:, cols] = (t[0:128] * (1.0 / math.sqrt(128))).astype(BF)
            dv_ref[:, cols] = t[128:256].astype(BF)


def rows_kernel(s_ref, oo0, oo1, dq0, dq1, r0, r1, tally_ref, out_ref, dq_ref):
    core = s_ref[0]
    scale = (4.0 * 4096) / tally_ref[0:1, 0:1]
    for j, (o, d, r) in enumerate(((oo0, dq0, r0), (oo1, dq1, r1))):
        mine = pl.ds(pl.multiple_of(core * 2048 + j * 1024, 128), 1024)
        theirs = pl.ds(pl.multiple_of((1 - core) * 2048 + j * 1024, 128), 1024)
        out_ref[:, mine] = o[...]
        out_ref[:, theirs] = r[0]
        dq_ref[:, mine] = (d[...].astype(F32) * scale).astype(BF)
        dq_ref[:, theirs] = (r[1].astype(F32) * scale).astype(BF)


def shard(queries, keys, values, out_grad, segment_ids, loss_mask):
    me = lax.axis_index("ctx")
    core, y, z = me & 1, (me >> 1) & 3, me >> 3
    q, k, v, g = queries[0], keys[0], values[0], out_grad[0]

    def send(x, target, turn=False):
        pairs = []
        for i in range(32):
            zz, yy, cc = target(i // 8, i // 2 % 4, i % 2)
            if turn or 0 <= zz < 4:
                pairs.append((i, (zz % 4 * 4 + yy % 4) * 2 + cc % 2))
        return lax.ppermute(x, "ctx", pairs)

    swap = lambda x: send(x, lambda z, y, c: (z, y, c + 1))
    along_z = lambda x, a, turn=False: send(x, lambda z, y, c: (z + a, y, c), turn)
    rows_of_y = [[(zz * 4 + yy) * 2 + cc for yy in range(4)] for zz in range(4) for cc in range(2)]
    trade_y = lambda x: lax.all_to_all(x, "ctx", 0, 0, axis_index_groups=rows_of_y)

    info = jnp.concatenate([segment_ids.astype(BF), loss_mask.astype(BF), jnp.zeros((14, 128), BF)], axis=0)

    def payload(c):
        heads = lambda a: lax.dynamic_slice(a, (0, c * 256), (128, 256)).reshape(128, 2, 128).transpose(1, 0, 2)
        return jnp.concatenate([heads(k), heads(v), jnp.broadcast_to(info, (2, 16, 128))], axis=1)

    own = jnp.stack([payload(core), swap(payload(1 - core))], axis=1)
    half = lambda a: lax.dynamic_slice(a, (0, (1 - core) * 2048), (128, 2048))
    qs, gs = swap(half(q)), swap(half(g))
    za, zc = along_z(own, 1, True), along_z(own, 2)
    scal = jnp.stack([core, z, y]).astype(jnp.int32)

    counted = jnp.broadcast_to(jnp.sum(za[0][:, 257].astype(F32)), (8, 128))
    for step in (1, 2):
        counted = counted + lax.ppermute(counted, "dp", [(i, i ^ step) for i in range(4)])

    kind = jax.ShapeDtypeStruct
    four = kind((4, 2, 2, 272, 128), BF)
    ys = [
        trade_y(small(spread_kernel, scal, (own, za, zc, n), [four], "spread", head=j)[0])
        for j, n in enumerate((jnp.zeros((8, 128), F32), counted))
    ]

    to = lambda x, a, c: send(x, lambda z, yy, cc: (z + a, yy, cc + c))
    oo0, dq0, pair0, part0, loc0, _ = attend(scal, 0, q, qs, g, gs, own, za, zc, ys[0], counted)
    got0 = trade_y(part0)
    oo1, dq1, pair1, part1, loc1, tally = attend(scal, 1, q, qs, g, gs, own, za, zc, ys[1], counted)
    sides, sides32 = kind((2, 256, 128), BF), kind((2, 256, 128), F32)
    a_mine, a_theirs, c_mine, c_theirs, here, here_theirs = small(
        sum_kernel, scal, (got0, loc0, trade_y(part1), loc1), [sides] * 4 + [sides32, sides], "sum"
    )
    kv = (here, to(a_mine, -1, 0), to(c_mine, -2, 0), swap(here_theirs), to(a_theirs, -1, 1), to(c_theirs, -2, 1))
    for step in (1, 2):
        tally = tally + send(tally, lambda z, y, c: (z ^ step, y, c))
    wide = kind((128, 4096), BF)
    attn, dq = small(rows_kernel, scal, (oo0, oo1, dq0, dq1, swap(pair0), swap(pair1), tally), [wide] * 2, "rows")
    dk, dv = small(final_kernel, scal, (tally, *kv), [kind((128, 512), BF)] * 2, "final")
    return attn[None], dq[None], dk[None], dv[None]


def solution(mesh):
    rows, ids = P("dp", "ctx", None), P("dp", "ctx")
    return jax.shard_map(
        shard, mesh=mesh, in_specs=(rows,) * 4 + (ids,) * 2, out_specs=(rows,) * 4, check_vma=False
    )
```

```python
import math, functools
import jax, jax.numpy as jnp
from jax import lax
from jax.sharding import PartitionSpec as P
from jax.experimental import pallas as pl
from jax.experimental.pallas import tpu as pltpu

NEG = -1e30
CH = math.log2(math.e) / math.sqrt(128)
BF, F32 = jnp.bfloat16, jnp.float32
NB = 9
NT = (((1,), (1,)), ((), ()))


def mm(a, b):
    return jnp.dot(a, b, preferred_element_type=F32)


def mmt(a, b):
    return lax.dot_general(a, b, NT, preferred_element_type=F32)


def run_heads(score, weigh, output, dscore, dvalue, dkey, dquery, start):
    R = range(NB)

    def pair(i, _):
        S = [start(2 * i), start(2 * i + 1)]
        for t in (0, 1):
            for b in R:
                score(t, S[t], b)
        for t in (0, 1):
            for b in R:
                weigh(t, S[t], b)
        for t in (0, 1):
            output(t, S[t])
        for t in (0, 1):
            for b in R:
                dscore(t, S[t], b)
        for t in (0, 1):
            for b in R:
                dvalue(t, S[t], b)
        for t in (0, 1):
            for b in R:
                dkey(t, S[t], b)
        for t in (0, 1):
            dquery(t, S[t])
        return 0

    lax.fori_loop(0, 4, pair, 0)


def run_ahead(score, weigh, output, dscore, dvalue, dkey, dquery, start):
    R = range(NB)
    S = [start(h) for h in range(8)]
    for b in R:
        score(0, S[0], b)
    for b in R:
        weigh(0, S[0], b)
    for b in R:
        score(1, S[1], b)
    for h in range(8):
        t, u = h % 2, (h + 1) % 2
        output(t, S[h])
        for b in R:
            dscore(t, S[h], b)
            if h < 7:
                weigh(u, S[h + 1], b)
        for b in R:
            dvalue(t, S[h], b)
            dkey(t, S[h], b)
            if h < 6:
                score(t, S[h + 2], b)
        dquery(t, S[h])


def attend_kernel(ahead, s_ref, qo_ref, qs_ref, go_ref, gs_ref, own_ref, za_ref, zc_ref, y_ref, tally_ref,
                  oo_ref, dqo_ref, swap_ref, *refs):
    n_parts = 1 if ahead else 3
    p_refs = refs[:n_parts]
    loc_ref, cnt_ref, kk, vv, kt, vt, bias, sc, pp, ds, dka, dva = refs[n_parts:]
    core, z, y = s_ref[0], s_ref[1], s_ref[2]
    chip = 4 * z + y
    blocks = [(own_ref, (), None), (za_ref, (), chip - 4), (zc_ref, (), chip - 8)]
    for s in (1, 2, 3):
        turned = (y - s) & 3
        blocks.append((y_ref, (turned, 0), 4 * z - 4 + turned))
        blocks.append((y_ref, (turned, 1), chip - s - jnp.where(y >= s, 0, 4)))
    lane = lax.broadcasted_iota(jnp.int32, (1, 128), 1)
    t_seg = jnp.concatenate([own_ref[0, 256:257], own_ref[1, 256:257]], axis=1).astype(F32)
    t_mask = jnp.concatenate([own_ref[0, 257:258], own_ref[1, 257:258]], axis=1).astype(F32)
    t_pos = jnp.concatenate([core * 128 + lane, (1 - core) * 128 + lane], axis=1)
    key = lax.broadcasted_iota(jnp.int32, (128, 256), 0)
    for b, (ref, pre, idx) in enumerate(blocks):
        for o in range(2):
            r0 = b * 256 + o * 128
            k = ref[pre + (o, slice(0, 128))]
            v = ref[pre + (o, slice(128, 256))]
            kk[r0:r0 + 128] = k
            vv[r0:r0 + 128] = v
            kt[:, r0:r0 + 128] = k.T
            vt[:, r0:r0 + 128] = v.T
            k_seg = ref[pre + (o, slice(256, 257))].astype(F32)
            n = [jnp.sum((k_seg < s).astype(F32), axis=1, keepdims=True) for s in (1, 2, 3)]
            first = jnp.where(t_seg == 3, n[2], jnp.where(t_seg == 2, n[1], jnp.where(t_seg == 1, n[0], 0.0)))
            first = first.astype(jnp.int32)
            if idx is None:
                at = core * 128 if o == 0 else (1 - core) * 128
                ok = (key >= first) & (key + at <= t_pos)
            else:
                first = jnp.where(idx >= 0, first, 128)
                ok = key >= first
            bias[r0:r0 + 128] = jnp.where(ok, 0.0, NEG)
    dka[...] = jnp.zeros_like(dka)
    dva[...] = jnp.zeros_like(dva)

    def load(h):
        cols = pl.ds(pl.multiple_of(h * 128, 128), 128)
        q = jnp.concatenate([qo_ref[:, cols], qs_ref[:, cols]], axis=0)
        g = jnp.concatenate([go_ref[:, cols], gs_ref[:, cols]], axis=0)
        return cols, q, g

    def score(t, st, b):
        rows = slice(b * 256, b * 256 + 256)
        s = mmt(kk[rows], st["q"]) + bias[rows]
        sc[t, rows] = s
        top = jnp.max(s.reshape(32, 8, 256), axis=0)
        st["top"] = top if b == 0 else jnp.maximum(st["top"], top)

    def weigh(t, st, b):
        if b == 0:
            st["top"] = jnp.max(st["top"], axis=0, keepdims=True) * CH
        rows = slice(b * 256, b * 256 + 256)
        p = jnp.exp2(sc[t, rows] * CH - st["top"])
        part = jnp.sum(p.reshape(32, 8, 256), axis=0)
        st["mass"] = part if b == 0 else st["mass"] + part
        pp[t, rows] = p.astype(BF)

    def output(t, st):
        inv = 1.0 / jnp.sum(st["mass"], axis=0, keepdims=True)
        ot = (mm(vt[...], pp[t]) * inv).astype(BF)
        out = ot.T
        oo_ref[:, st["cols"]] = out[:128]
        swap_ref[0, :, st["cols"]] = out[128:]
        st["delta"] = jnp.sum(ot.astype(F32) * st["g"].T.astype(F32), axis=0, keepdims=True)
        st["inv"] = inv * t_mask
        col = jnp.broadcast_to(st["inv"], (128, 256)).T
        st["qn"] = (st["q"].astype(F32) * col).astype(BF)
        st["gn"] = (st["g"].astype(F32) * col).astype(BF)

    def dscore(t, st, b):
        rows = slice(b * 256, b * 256 + 256)
        ds[t, rows] = (pp[t, rows].astype(F32) * (mmt(vv[rows], st["g"]) - st["delta"])).astype(BF)

    def dvalue(t, st, b):
        rows = slice(b * 256, b * 256 + 256)
        dva[rows] += mm(pp[t, rows], st["gn"])

    def dkey(t, st, b):
        rows = slice(b * 256, b * 256 + 256)
        dka[rows] += mm(ds[t, rows], st["qn"])

    def dquery(t, st):
        dq = (mm(kt[...], ds[t]) * (st["inv"] * (1.0 / math.sqrt(128)))).astype(BF).T
        dqo_ref[:, st["cols"]] = dq[:128]
        swap_ref[1, :, st["cols"]] = dq[128:]

    def start(h):
        st = {}
        st["cols"], st["q"], st["g"] = load(h)
        return st

    (run_ahead if ahead else run_heads)(score, weigh, output, dscore, dvalue, dkey, dquery, start)
    tally = tally_ref[...]
    for s in (1, 2, 3):
        digits = y_ref[(y - s) & 3, 0, 0, 256:272].astype(F32)
        tally = tally + 32.0 * digits[2:3] + digits[3:4]
    cnt_ref[...] = tally
    for b in range(NB):
        for o in range(2):
            rows = slice(b * 256 + o * 128, b * 256 + o * 128 + 128)
            if b < 3:
                loc_ref[b, o, 0:128] = dka[rows]
                loc_ref[b, o, 128:256] = dva[rows]
            else:
                s = (b - 1) // 2
                ref, at = (p_refs[0], ((y - s) & 3,)) if ahead else (p_refs[s - 1], ())
                ref[at + ((b - 3) % 2, o, slice(0, 128))] = dka[rows].astype(BF)
                ref[at + ((b - 3) % 2, o, slice(128, 256))] = dva[rows].astype(BF)


def whole(a):
    return pl.BlockSpec(a.shape, lambda i, s, n=len(a.shape): (0,) * n)


def of_head(j):
    return pl.BlockSpec((None, 2, 272, 128), lambda i, s: (j, 0, 0, 0))


def attend(scal, j, q, qs, g, gs, own, za, zc, ys, tally):
    wide = lambda f: pl.BlockSpec((128, 1024), f)
    mine = wide(lambda i, s: (0, s[0] * 2 + j))
    other = wide(lambda i, s: (0, j))
    rows = jax.ShapeDtypeStruct((128, 1024), BF)
    pair = jax.ShapeDtypeStruct((2, 128, 1024), BF)
    loc = jax.ShapeDtypeStruct((3, 2, 256, 128), F32)
    part = jax.ShapeDtypeStruct((2, 2, 256, 128), BF)
    parts = [jax.ShapeDtypeStruct((4, 2, 2, 256, 128), BF)] if j else [part] * 3
    outs = [rows, rows, pair, *parts, loc, jax.ShapeDtypeStruct((8, 128), F32)]
    n = NB * 256
    ins = (own, za, zc, ys, tally)
    return pl.pallas_call(
        functools.partial(attend_kernel, j == 1),
        out_shape=outs,
        grid_spec=pltpu.PrefetchScalarGridSpec(
            num_scalar_prefetch=1,
            grid=(1,),
            in_specs=[mine, other, mine, other] + [of_head(j)] * 3 + [whole(ys), whole(tally)],
            out_specs=[whole(o) for o in outs],
            scratch_shapes=[
                pltpu.VMEM((n, 128), BF), pltpu.VMEM((n, 128), BF), pltpu.VMEM((128, n), BF), pltpu.VMEM((128, n), BF),
                pltpu.VMEM((n, 256), F32), pltpu.VMEM((2, n, 256), F32), pltpu.VMEM((2, n, 256), BF),
                pltpu.VMEM((2, n, 256), BF), pltpu.VMEM((n, 128), F32), pltpu.VMEM((n, 128), F32),
            ],
        ),
        compiler_params=pltpu.CompilerParams(vmem_limit_bytes=60 * 2**20),
        cost_estimate=pl.CostEstimate(flops=15 * 2**30, bytes_accessed=4 * 2**20, transcendentals=5 * 2**20),
        name="attend",
    )(scal, q, qs, g, gs, *ins)


def small(kernel, scal, ins, outs, name, head=None):
    return pl.pallas_call(
        kernel,
        out_shape=outs,
        grid_spec=pltpu.PrefetchScalarGridSpec(
            num_scalar_prefetch=1,
            grid=(1,),
            in_specs=[of_head(head) if len(a.shape) == 4 and head is not None else whole(a) for a in ins],
            out_specs=[whole(o) for o in outs],
        ),
        compiler_params=pltpu.CompilerParams(vmem_limit_bytes=16 * 2**20),
        name=name,
    )(scal, *ins)


def spread_kernel(s_ref, own_ref, za_ref, zc_ref, tally_ref, out_ref):
    y = s_ref[2]
    tally = tally_ref[...]
    high = jnp.floor(tally * (1 / 32))
    row = lax.broadcasted_iota(jnp.int32, (16, 128), 0)
    info = za_ref[0, 256:272].astype(F32)
    info = jnp.where(row == 2, high[:1], jnp.where(row == 3, (tally - 32 * high)[:1], info)).astype(BF)
    for t in range(4):
        out_ref[t, 0] = za_ref[...]
        out_ref[t, 0, 0, 256:272] = info

        @pl.when(y < t)
        def _():
            out_ref[t, 1] = own_ref[...]

        @pl.when(y >= t)
        def _():
            out_ref[t, 1] = zc_ref[...]


def sum_kernel(s_ref, got01, got02, got03, loc0, got1, loc1, a_mine, a_theirs, c_mine, c_theirs, here, here_theirs):
    y = s_ref[2]
    for j, (got, loc_ref) in enumerate((((got01, got02, got03), loc0), (got1, loc1))):
        a, c, h = loc_ref[1], loc_ref[2], loc_ref[0]
        for s in (1, 2, 3):
            at = ((y + s) & 3,) if j else ()
            r = got if j else got[s - 1]
            a = a + r[at + (0,)].astype(F32)
            b = r[at + (1,)].astype(F32)
            h = h + jnp.where(y + s < 4, b, 0.0)
            c = c + jnp.where(y + s < 4, 0.0, b)
        a_mine[j] = a[0].astype(BF)
        a_theirs[j] = a[1].astype(BF)
        c_mine[j] = c[0].astype(BF)
        c_theirs[j] = c[1].astype(BF)
        here[j] = h[0]
        here_theirs[j] = h[1].astype(BF)


def final_kernel(s_ref, tally_ref, *refs):
    core = s_ref[0]
    dk_ref, dv_ref = refs[6:]
    scale = (4.0 * 4096) / tally_ref[0:1]
    for j in range(2):
        for c, three in ((core, refs[:3]), (1 - core, refs[3:6])):
            t = sum(r[j].astype(F32) for r in three) * scale
            cols = pl.ds(pl.multiple_of(c * 256 + j * 128, 128), 128)
            dk_ref[:, cols] = (t[0:128] * (1.0 / math.sqrt(128))).astype(BF)
            dv_ref[:, cols] = t[128:256].astype(BF)


def rows_kernel(s_ref, oo0, oo1, dq0, dq1, r0, r1, tally_ref, out_ref, dq_ref):
    core = s_ref[0]
    scale = (4.0 * 4096) / tally_ref[0:1, 0:1]
    for j, (o, d, r) in enumerate(((oo0, dq0, r0), (oo1, dq1, r1))):
        mine = pl.ds(pl.multiple_of(core * 2048 + j * 1024, 128), 1024)
        theirs = pl.ds(pl.multiple_of((1 - core) * 2048 + j * 1024, 128), 1024)
        out_ref[:, mine] = o[...]
        out_ref[:, theirs] = r[0]
        dq_ref[:, mine] = (d[...].astype(F32) * scale).astype(BF)
        dq_ref[:, theirs] = (r[1].astype(F32) * scale).astype(BF)


def shard(queries, keys, values, out_grad, segment_ids, loss_mask):
    me = lax.axis_index("ctx")
    core, y, z = me & 1, (me >> 1) & 3, me >> 3
    q, k, v, g = queries[0], keys[0], values[0], out_grad[0]

    def send(x, target, turn=False):
        pairs = []
        for i in range(32):
            zz, yy, cc = target(i // 8, i // 2 % 4, i % 2)
            if turn or 0 <= zz < 4:
                pairs.append((i, (zz % 4 * 4 + yy % 4) * 2 + cc % 2))
        return lax.ppermute(x, "ctx", pairs)

    swap = lambda x: send(x, lambda z, y, c: (z, y, c + 1))
    along_z = lambda x, a, turn=False: send(x, lambda z, y, c: (z + a, y, c), turn)
    rows_of_y = [[(zz * 4 + yy) * 2 + cc for yy in range(4)] for zz in range(4) for cc in range(2)]
    trade_y = lambda x: lax.all_to_all(x, "ctx", 0, 0, axis_index_groups=rows_of_y)

    info = jnp.concatenate([segment_ids.astype(BF), loss_mask.astype(BF), jnp.zeros((14, 128), BF)], axis=0)

    def payload(c):
        heads = lambda a: lax.dynamic_slice(a, (0, c * 256), (128, 256)).reshape(128, 2, 128).transpose(1, 0, 2)
        return jnp.concatenate([heads(k), heads(v), jnp.broadcast_to(info, (2, 16, 128))], axis=1)

    own = jnp.stack([payload(core), swap(payload(1 - core))], axis=1)
    half = lambda a: lax.dynamic_slice(a, (0, (1 - core) * 2048), (128, 2048))
    qs, gs = swap(half(q)), swap(half(g))
    za, zc = along_z(own, 1, True), along_z(own, 2)
    scal = jnp.stack([core, z, y]).astype(jnp.int32)

    counted = jnp.broadcast_to(jnp.sum(za[0][:, 257].astype(F32)), (8, 128))
    for step in (1, 2):
        counted = counted + lax.ppermute(counted, "dp", [(i, i ^ step) for i in range(4)])

    kind = jax.ShapeDtypeStruct
    four = kind((4, 2, 2, 272, 128), BF)
    ys = [
        trade_y(small(spread_kernel, scal, (own, za, zc, n), [four], "spread", head=j)[0])
        for j, n in enumerate((jnp.zeros((8, 128), F32), counted))
    ]

    to = lambda x, a, c: send(x, lambda z, yy, cc: (z + a, yy, cc + c))
    oo0, dq0, pair0, *parts, loc0, _ = attend(scal, 0, q, qs, g, gs, own, za, zc, ys[0], counted)
    got0 = [send(p, lambda z, y, c: (z, y - s, c)) for s, p in zip((1, 2, 3), parts)]
    oo1, dq1, pair1, part1, loc1, tally = attend(scal, 1, q, qs, g, gs, own, za, zc, ys[1], counted)
    sides, sides32 = kind((2, 256, 128), BF), kind((2, 256, 128), F32)
    a_mine, a_theirs, c_mine, c_theirs, here, here_theirs = small(
        sum_kernel, scal, (*got0, loc0, trade_y(part1), loc1), [sides] * 4 + [sides32, sides], "sum"
    )
    kv = (here, to(a_mine, -1, 0), to(c_mine, -2, 0), swap(here_theirs), to(a_theirs, -1, 1), to(c_theirs, -2, 1))
    for step in (1, 2):
        tally = tally + send(tally, lambda z, y, c: (z ^ step, y, c))
    wide = kind((128, 4096), BF)
    attn, dq = small(rows_kernel, scal, (oo0, oo1, dq0, dq1, swap(pair0), swap(pair1), tally), [wide] * 2, "rows")
    dk, dv = small(final_kernel, scal, (tally, *kv), [kind((128, 512), BF)] * 2, "final")
    return attn[None], dq[None], dk[None], dv[None]


def solution(mesh):
    rows, ids = P("dp", "ctx", None), P("dp", "ctx")
    return jax.shard_map(
        shard, mesh=mesh, in_specs=(rows,) * 4 + (ids,) * 2, out_specs=(rows,) * 4, check_vma=False
    )
```
